32 devices in a mesh: mode: 4 (over y, x), cell: 8 (over z, core).
Axes of the slice: x: 2, y: 2, z: 4, core: 2. Of those that a mesh axis runs over, the one named last changes fastest.
Arguments:
- populations: float32 [2048, 1, 16, 128], P('mode', None, 'cell'), may hold values from -6 to 6
- contact_mask: int32 [1, 16, 128], P(None, 'cell'), may hold values 0 or 1
- octant: int32 [2048], P('mode'), may hold values from 0 to 7
- courant: float32 [3, 2048], P(None, 'mode'), may hold values from 0.03 to 0.3
- collision: bfloat16 [2048, 2048], P('mode'), as said below
Outputs:
- advanced: float32 [2048, 1, 16, 128], P('mode', None, 'cell')
The draws below stay inside these ranges and needn't reach their ends.
Inputs may be any that keep to these rules, and one draw needn't show every extreme that they name: `collision`: diagonal entries between 0.1 and 0.6, off-diagonal ones small, all independent.
All inputs are finite; a program needn't handle non-finite values. No bound on the sum of `contact_mask` on one device may be relied on, other than what follows from the above.
Results may differ from the reference program's by a relative error of at most 0.0014.
Values may be sent and summed in bfloat16 or wider, within the bound.
No kernel may reach another device: no remote copies, remote signals or barrier semaphores. Data moves between devices by JAX's collectives and lax.ppermute only.
A program may use at most 64 MiB of HBM per device.

```python
import math
import jax
import jax.numpy as jnp

MODES = 2048
PLANES = 1
NX = 128
NY = 16


def draw_collision(key, part):
    key_diag = jax.random.fold_in(key, 11)
    key_off = jax.random.fold_in(key, 12)
    diag = jax.random.uniform(key_diag, (MODES,), jnp.float32, 0.1, 0.6)
    off = jax.random.normal(key_off, (MODES, MODES), jnp.float32)
    off = off * (0.2 / math.sqrt(MODES))
    eye = jnp.eye(MODES, dtype=jnp.float32)
    return (off * (1.0 - eye) + eye * diag[:, None]).astype(jnp.bfloat16)


def with_ends(drawn, stream_key, least, high):
    place = [jax.random.randint(jax.random.fold_in(stream_key, axis), (), 0, length) for axis, length in enumerate(drawn.shape)]
    longest = drawn.shape.index(max(drawn.shape))
    beside = place[:longest] + [(place[longest] + 1) % drawn.shape[longest]] + place[longest + 1:]
    return drawn.at[tuple(place)].set(least).at[tuple(beside)].set(high)


def levels(stream_key, shape, shards, least, top_value):
    loudness = 1.0
    for position, blocks in shards:
        steps = jax.random.uniform(jax.random.fold_in(jax.random.fold_in(stream_key, 6), position), (blocks,), jnp.float32, least / len(shards), top_value / len(shards))
        loudness = loudness * jnp.repeat(jnp.exp(steps), shape[position] // blocks).reshape((-1,) + (1,) * (len(shape) - 1 - position))
    return loudness


def normal_values(key, extent, width, reach, split=(), kind=jnp.bfloat16):
    level = levels(key, extent, split, -0.22, 0.18) if split else 1.0
    drawn = jax.random.normal(key, extent, jnp.float32) * width * level
    return jnp.minimum(jnp.maximum(drawn, -reach), reach).astype(kind)


def setup_inputs(seed: int = 0) -> dict:
    key_of = jax.random.split(jax.random.key(seed), 6)
    return {
        "populations": normal_values(key_of[0], (MODES, PLANES, NY, NX), 1.0, 6.0, ((0, 4), (2, 8)), jnp.float32),
        "contact_mask": with_ends((jax.random.randint(key_of[1], (PLANES, NY, NX), 0, 8) < 1).astype(jnp.int32), jax.random.fold_in(key_of[1], 1), 0, 1),
        "octant": with_ends(jax.random.randint(key_of[2], (MODES,), 0, 8), jax.random.fold_in(key_of[2], 1), 0, 7).astype(jnp.int32),
        "courant": jnp.clip(jnp.exp(math.log(0.3) - 2.3025852 * jax.random.uniform(key_of[3], (3, MODES), jnp.float32) ** levels(key_of[3], (3, MODES), ((1, 4),), -0.2, 0.2)), 0.03, 0.3),
        "collision": draw_collision(jax.random.fold_in(key_of[5], 71), 0),
    }


def velocities(octant, courant):
    bits = [octant % 2, (octant // 2) % 2, (octant // 4) % 2]
    return [(1.0 - 2.0 * bits[d].astype(jnp.float32)) * courant[d] for d in range(3)]


def advect(field, speeds):
    vx, vy, vz = [s[:, None, None, None] for s in speeds]
    back_x = jnp.roll(field, 1, axis=3)
    ahead_x = jnp.roll(field, -1, axis=3)
    padded_y = jnp.pad(field, ((0, 0), (0, 0), (1, 1), (0, 0)))
    padded_z = jnp.pad(field, ((0, 0), (1, 1), (0, 0), (0, 0)))
    total = jnp.maximum(vx, 0.0) * (field - back_x) + jnp.minimum(vx, 0.0) * (ahead_x - field)
    total = total + jnp.maximum(vy, 0.0) * (field - padded_y[:, :, :-2]) + jnp.minimum(vy, 0.0) * (padded_y[:, :, 2:] - field)
    total = total + jnp.maximum(vz, 0.0) * (field - padded_z[:, :-2]) + jnp.minimum(vz, 0.0) * (padded_z[:, 2:] - field)
    return total


def collide(field, collision):
    rounded = field.astype(jnp.bfloat16).reshape(field.shape[0], -1)
    return jnp.dot(collision, rounded, preferred_element_type=jnp.float32).reshape(field.shape)


def reference(populations, contact_mask, octant, courant, collision):
    keep = (1 - contact_mask).astype(jnp.float32)[None]
    speeds = velocities(octant, courant)
    first = keep * populations
    second = keep * (first - advect(first, speeds) - collide(first, collision))
    final = second - advect(second, speeds) - collide(second, collision)
    return keep * (0.5 * first + 0.5 * final)
```

```python
import functools

import jax
import jax.numpy as jnp
from jax import lax
from jax.experimental import pallas as pl
from jax.experimental.pallas import tpu as pltpu
from jax.sharding import PartitionSpec as P

F32 = jnp.float32
BF16 = jnp.bfloat16
VMEM = pl.BlockSpec(memory_space=pltpu.VMEM)


def call(body, outs, args, flops=0):
    total = sum(a.size * a.dtype.itemsize for a in (*outs, *args))
    return pl.pallas_call(
        body,
        out_shape=outs,
        in_specs=[VMEM] * len(args),
        out_specs=[VMEM] * len(outs),
        compiler_params=pltpu.CompilerParams(vmem_limit_bytes=24 * 2**20),
        cost_estimate=pl.CostEstimate(flops=flops, bytes_accessed=total, transcendentals=0),
    )(*args)


def shape(dims, dtype):
    return jax.ShapeDtypeStruct(dims, dtype)


def masked_rows(pop_ref, mask_ref, rows):
    modes = pop_ref.shape[0] // rows
    keep = (1 - mask_ref[...]).astype(F32)
    return [keep[r : r + 1] * pop_ref[pl.ds(r, modes, stride=rows), :] for r in range(rows)]


def prepare(rows, pop_ref, mask_ref, octant_ref, courant_ref, *outs):
    *q_refs, coef_ref = outs
    for q_ref, row in zip(q_refs, masked_rows(pop_ref, mask_ref, rows)):
        q_ref[...] = row.astype(BF16)
    octant = octant_ref[...]
    signs = [1.0 - 2.0 * ((octant >> d) & 1).astype(F32) for d in range(3)]
    speeds = [signs[d] * courant_ref[d : d + 1] for d in range(3)]
    table = jnp.concatenate(
        [jnp.abs(v) for v in speeds] + [(v < 0).astype(F32) for v in speeds] + [speeds[0] * 0.0] * 2, axis=0
    )
    coef_ref[...] = table.T


def product(c_ref, offset, blocks):
    modes = blocks[0].shape[0]
    position = lax.axis_index("mode") ^ offset
    columns = pl.ds(pl.multiple_of(position * modes, modes), modes)
    return jnp.dot(c_ref[:, columns], jnp.concatenate(blocks, axis=1), preferred_element_type=F32)


def local_terms(rows, fields, q_refs, coef_ref, c_ref):
    width = fields[0].shape[1]
    ax, ay, az = (coef_ref[:, d : d + 1] for d in range(3))
    neg_x, neg_y = (coef_ref[:, d : d + 1] > 0 for d in (3, 4))
    own = product(c_ref, 0, [q[...] for q in q_refs])
    stay = 1.0 - (ax + ay + az)
    results = []
    for r, p in enumerate(fields):
        beside = jnp.where(neg_x, pltpu.roll(p, width - 1, 1), pltpu.roll(p, 1, 1))
        low = fields[r - 1] if r > 0 else jnp.zeros_like(p)
        high = fields[r + 1] if r < rows - 1 else jnp.zeros_like(p)
        results.append(stay * p + ax * beside + ay * jnp.where(neg_y, high, low) - own[:, r * width : (r + 1) * width])
    return results


def remote_terms(rows, offsets, width, received, halos, coef_ref, c_ref):
    ay = coef_ref[:, 1:2]
    neg_y = coef_ref[:, 4:5] > 0
    low, high = (h[...].astype(F32) for h in halos)
    total = None
    for i, offset in enumerate(offsets):
        term = product(c_ref, offset, [received[r][i][...] for r in range(rows)])
        total = term if total is None else total + term
    results = [-total[:, r * width : (r + 1) * width] for r in range(rows)]
    results[0] = results[0] + jnp.where(neg_y, 0.0, ay * low)
    results[-1] = results[-1] + jnp.where(neg_y, ay * high, 0.0)
    return results


def first_local(rows, *refs):
    pop_ref, mask_ref, coef_ref, c_ref, *rest = refs
    q_refs, base_ref = rest[:rows], rest[rows]
    fields = masked_rows(pop_ref, mask_ref, rows)
    for r, value in enumerate(local_terms(rows, fields, q_refs, coef_ref, c_ref)):
        base_ref[r] = value


def first_end(rows, offsets, *refs):
    base_ref, mask_ref, coef_ref, c_ref, low, high, *rest = refs
    n = len(offsets)
    received = [rest[r * n : (r + 1) * n] for r in range(rows)]
    *q_refs, p1_ref = rest[rows * n :]
    keep = (1 - mask_ref[...]).astype(F32)
    width = keep.shape[1]
    for r, term in enumerate(remote_terms(rows, offsets, width, received, (low, high), coef_ref, c_ref)):
        value = keep[r : r + 1] * (base_ref[r] + term)
        p1_ref[r] = value
        q_refs[r][...] = value.astype(BF16)


def second_local(rows, *refs):
    pop_ref, mask_ref, p1_ref, coef_ref, c_ref, *rest = refs
    q_refs, base_ref = rest[:rows], rest[rows]
    first = masked_rows(pop_ref, mask_ref, rows)
    fields = [p1_ref[r] for r in range(rows)]
    for r, value in enumerate(local_terms(rows, fields, q_refs, coef_ref, c_ref)):
        base_ref[r] = 0.5 * first[r] + 0.5 * value


def second_end(rows, offsets, *refs):
    base_ref, mask_ref, coef_ref, c_ref, low, high, *rest = refs
    n = len(offsets)
    received = [rest[r * n : (r + 1) * n] for r in range(rows)]
    out_ref = rest[rows * n]
    keep = (1 - mask_ref[...]).astype(F32)
    width = keep.shape[1]
    modes = out_ref.shape[0] // rows
    for r, term in enumerate(remote_terms(rows, offsets, width, received, (low, high), coef_ref, c_ref)):
        out_ref[pl.ds(r, modes, stride=rows), :] = keep[r : r + 1] * (base_ref[r] + 0.5 * term)


def exchange(q, count):
    bits = [1 << b for b in range(count.bit_length() - 1)]
    gathered = []
    for r, row in enumerate(q):
        held = {0: row}
        for bit in bits if r % 2 == 0 else bits[::-1]:
            pairs = [(i, i ^ bit) for i in range(count)]
            held |= {o ^ bit: lax.ppermute(b, "mode", pairs) for o, b in held.items()}
        gathered.append(held)
    return gathered


def halo(q):
    count = lax.axis_size("cell")
    forward = [(i, i + 1) for i in range(count - 1)]
    backward = [(target, source) for source, target in forward]
    return lax.ppermute(q[-1], "cell", forward), lax.ppermute(q[0], "cell", backward)


def on_device(populations, contact_mask, octant, courant, collision):
    modes, planes, rows, width = populations.shape
    assert planes == 1
    count = lax.axis_size("mode")
    offsets = list(range(1, count))
    pop = populations.reshape(modes * rows, width)
    mask = contact_mask.reshape(rows, width)
    row_bf16 = shape((modes, width), BF16)
    all_rows = shape((rows, modes, width), F32)
    flops = 2 * modes * modes * rows * width

    *q, coef = call(
        functools.partial(prepare, rows),
        [row_bf16] * rows + [shape((modes, 8), F32)],
        [pop, mask, octant.reshape(1, modes), courant],
    )
    low, high = halo(q)
    gathered = exchange(q, count)
    (base,) = call(
        functools.partial(first_local, rows), [all_rows], [pop, mask, coef, collision, *q], flops=flops
    )
    blocks = [g[o] for g in gathered for o in offsets]
    *q, p1 = call(
        functools.partial(first_end, rows, offsets),
        [row_bf16] * rows + [all_rows],
        [base, mask, coef, collision, low, high, *blocks],
        flops=flops * len(offsets),
    )
    low, high = halo(q)
    gathered = exchange(q, count)
    (base,) = call(
        functools.partial(second_local, rows), [all_rows], [pop, mask, p1, coef, collision, *q], flops=flops
    )
    blocks = [g[o] for g in gathered for o in offsets]
    (out,) = call(
        functools.partial(second_end, rows, offsets),
        [shape((modes * rows, width), F32)],
        [base, mask, coef, collision, low, high, *blocks],
        flops=flops * len(offsets),
    )
    return out.reshape(populations.shape)


def solution(mesh):
    placed = (
        P("mode", None, "cell", None),
        P(None, "cell", None),
        P("mode"),
        P(None, "mode"),
        P("mode", None),
    )
    return jax.shard_map(
        on_device,
        mesh=mesh,
        in_specs=placed,
        out_specs=P("mode", None, "cell", None),
        check_vma=False,
    )
```

```python
import functools

import jax
import jax.numpy as jnp
from jax import lax
from jax.experimental import pallas as pl
from jax.experimental.pallas import tpu as pltpu
from jax.sharding import PartitionSpec as P

F32 = jnp.float32
BF16 = jnp.bfloat16
VMEM = pl.BlockSpec(memory_space=pltpu.VMEM)
HBM = pl.BlockSpec(memory_space=pltpu.HBM)


def call(body, outs, args, in_specs=None, out_specs=None, scratch=(), flops=0):
    total = sum(a.size * a.dtype.itemsize for a in (*outs, *args))
    return pl.pallas_call(
        body,
        out_shape=outs,
        in_specs=in_specs or [VMEM] * len(args),
        out_specs=out_specs or [VMEM] * len(outs),
        scratch_shapes=list(scratch),
        compiler_params=pltpu.CompilerParams(vmem_limit_bytes=24 * 2**20),
        cost_estimate=pl.CostEstimate(flops=flops, bytes_accessed=total, transcendentals=0),
    )(*args)


def shape(dims, dtype):
    return jax.ShapeDtypeStruct(dims, dtype)


def is_first():
    return 1 - lax.axis_index("cell") % 2


def source_row(r, rows):
    return r + is_first() * (rows - 1 - 2 * r)


def prepare(rows, pop_hbm, mask_hbm, octant_hbm, courant_hbm, *refs):
    q_refs, (p0_ref, keep_ref, coef_ref) = refs[:rows], refs[rows : rows + 3]
    pop_ref, mask_ref, octant_ref, courant_ref, sems = refs[rows + 3 :]
    pairs = (mask_hbm, mask_ref), (pop_hbm, pop_ref), (octant_hbm, octant_ref), (courant_hbm, courant_ref)
    copies = [pltpu.make_async_copy(*pair, sems.at[i]) for i, pair in enumerate(pairs)]
    for copy in copies:
        copy.start()
    modes = p0_ref.shape[1]
    copies[0].wait()
    copies[1].wait()
    for r in range(rows):
        source = source_row(r, rows)
        keep = (1 - mask_ref[pl.ds(source, 1), :]).astype(F32)
        row = keep * pop_ref[pl.ds(source, modes, stride=rows), :]
        keep_ref[r : r + 1, :] = keep
        p0_ref[r] = row
        q_refs[r][...] = row.astype(BF16)
    copies[2].wait()
    copies[3].wait()
    octant = octant_ref[...]
    speeds = [(1.0 - 2.0 * ((octant >> d) & 1).astype(F32)) * courant_ref[d : d + 1] for d in range(3)]
    flags = [(v < 0).astype(F32) for v in speeds]
    table = jnp.concatenate([jnp.abs(v) for v in speeds] + flags + flags[:2], axis=0)
    coef_ref[...] = table.T


def columns(offset, modes):
    position = lax.axis_index("mode") ^ offset
    return pl.ds(pl.multiple_of(position * modes, modes), modes)


def product(c_ref, offset, blocks):
    cols = columns(offset, blocks[0].shape[0])
    return jnp.dot(c_ref[:, cols], jnp.concatenate(blocks, axis=1), preferred_element_type=F32)


def backward_y(coef_ref):
    return (coef_ref[:, 4:5] > 0) == (is_first() == 0)


def near_terms(fields, q_refs, early, blocks, coef_ref, c_ref):
    rows = len(fields)
    modes, width = fields[0].shape
    ax, ay, az = (coef_ref[:, d : d + 1] for d in range(3))
    neg_x = coef_ref[:, 3:4] > 0
    after = backward_y(coef_ref)
    stay = 1.0 - (ax + ay + az)
    results = []
    for r, p in enumerate(fields):
        beside = jnp.where(neg_x, pltpu.roll(p, width - 1, 1), pltpu.roll(p, 1, 1))
        prior = fields[r - 1] if r > 0 else jnp.zeros_like(p)
        later = fields[r + 1] if r < rows - 1 else jnp.zeros_like(p)
        results.append(stay * p + ax * beside + ay * jnp.where(after, later, prior))
    total = product(c_ref, 0, [q[...] for q in q_refs])
    for i, offset in enumerate(early):
        total = total + product(c_ref, offset, [b[...] for b in blocks[i * rows : (i + 1) * rows]])
    return [v - total[:, r * width : (r + 1) * width] for r, v in enumerate(results)]


def far_terms(rows, late, blocks, inner, outer, coef_ref, c_ref):
    width = inner.shape[1]
    ay = coef_ref[:, 1:2]
    after = backward_y(coef_ref)
    results = [None] * rows
    if late:
        total = sum(
            product(c_ref, offset, [b[...] for b in blocks[i * rows : (i + 1) * rows]]) for i, offset in enumerate(late)
        )
        results = [-total[:, r * width : (r + 1) * width] for r in range(rows)]
    else:
        results = [jnp.zeros(inner.shape, F32)] * rows
    results[0] = results[0] + jnp.where(after, 0.0, ay * inner[...].astype(F32))
    results[-1] = results[-1] + jnp.where(after, ay * outer[...].astype(F32), 0.0)
    return results


def first_near(rows, early, *refs):
    p0_ref, coef_ref, c_hbm, *rest = refs
    q_refs, blocks = rest[:rows], rest[rows : rows * (1 + len(early))]
    base_ref, c_ref, sem = rest[rows * (1 + len(early)) :]
    copy = pltpu.make_async_copy(c_hbm, c_ref, sem)
    copy.start()
    copy.wait()
    for r, value in enumerate(near_terms([p0_ref[r] for r in range(rows)], q_refs, early, blocks, coef_ref, c_ref)):
        base_ref[r] = value


def first_end(rows, late, *refs):
    base_ref, keep_ref, coef_ref, c_ref, inner, outer, *rest = refs
    blocks, (*q_refs, p1_ref) = rest[: rows * len(late)], rest[rows * len(late) :]
    for r, term in enumerate(far_terms(rows, late, blocks, inner, outer, coef_ref, c_ref)):
        value = keep_ref[r : r + 1] * (base_ref[r] + term)
        p1_ref[r] = value
        q_refs[r][...] = value.astype(BF16)


def second_near(rows, early, *refs):
    p0_ref, p1_ref, coef_ref, c_ref, *rest = refs
    q_refs, blocks, base_ref = rest[:rows], rest[rows:-1], rest[-1]
    for r, value in enumerate(near_terms([p1_ref[r] for r in range(rows)], q_refs, early, blocks, coef_ref, c_ref)):
        base_ref[r] = 0.5 * p0_ref[r] + 0.5 * value


def second_end(rows, late, *refs):
    base_ref, keep_ref, coef_ref, c_ref, inner, outer, *rest = refs
    blocks, out_ref = rest[:-1], rest[-1]
    modes = out_ref.shape[0] // rows
    for r, term in enumerate(far_terms(rows, late, blocks, inner, outer, coef_ref, c_ref)):
        out_ref[pl.ds(source_row(r, rows), modes, stride=rows), :] = keep_ref[r : r + 1] * (base_ref[r] + 0.5 * term)


def exchange(q, count):
    bits = [1 << b for b in range(count.bit_length() - 1)]
    gathered = [{0: row} for row in q]
    orders = [bits if r % 2 == 0 else bits[::-1] for r in range(len(q))]
    for step in range(len(bits)):
        for held, order in zip(gathered, orders):
            bit = order[step]
            pairs = [(i, i ^ bit) for i in range(count)]
            held |= {o ^ bit: lax.ppermute(b, "mode", pairs) for o, b in held.items()}
    return gathered


def halo(q):
    count = lax.axis_size("cell")
    within = [(i, i ^ 1) for i in range(count)]
    between = [(i, i + 1) for i in range(1, count - 1, 2)]
    between += [(target, source) for source, target in between]
    return lax.ppermute(q[0], "cell", within), lax.ppermute(q[-1], "cell", between)


def on_device(populations, contact_mask, octant, courant, collision):
    modes, planes, rows, width = populations.shape
    count = lax.axis_size("mode")
    assert planes == 1 and lax.axis_size("cell") % 2 == 0 and count & (count - 1) == 0
    early = [1 << b for b in range(count.bit_length() - 1)]
    late = [o for o in range(1, count) if o not in early]
    pop = populations.reshape(modes * rows, width)
    mask = contact_mask.reshape(rows, width)
    octant = octant.reshape(1, modes)
    row_bf16 = shape((modes, width), BF16)
    all_rows = shape((rows, modes, width), F32)
    flops = 2 * modes * modes * rows * width
    near = flops * (1 + len(early))
    far = flops * len(late)

    *q, p0, keep, coef = call(
        functools.partial(prepare, rows),
        [row_bf16] * rows + [all_rows, shape((rows, width), F32), shape((modes, 8), F32)],
        [pop, mask, octant, courant],
        in_specs=[HBM] * 4,
        scratch=[pltpu.VMEM(a.shape, a.dtype) for a in (pop, mask, octant, courant)] + [pltpu.SemaphoreType.DMA((4,))],
    )
    gathered = exchange(q, count)
    inner, outer = halo(q)
    args = [p0, coef, collision, *q, *(g[o] for o in early for g in gathered)]
    base, c = call(
        functools.partial(first_near, rows, early),
        [all_rows, shape(collision.shape, collision.dtype)],
        args,
        in_specs=[VMEM, VMEM, HBM] + [VMEM] * (len(args) - 3),
        scratch=[pltpu.SemaphoreType.DMA],
        flops=near,
    )
    *q, p1 = call(
        functools.partial(first_end, rows, late),
        [row_bf16] * rows + [all_rows],
        [base, keep, coef, c, inner, outer, *(g[o] for o in late for g in gathered)],
        flops=far,
    )
    gathered = exchange(q, count)
    inner, outer = halo(q)
    (base,) = call(
        functools.partial(second_near, rows, early),
        [all_rows],
        [p0, p1, coef, c, *q, *(g[o] for o in early for g in gathered)],
        flops=near,
    )
    (out,) = call(
        functools.partial(second_end, rows, late),
        [shape((modes * rows, width), F32)],
        [base, keep, coef, c, inner, outer, *(g[o] for o in late for g in gathered)],
        flops=far,
    )
    return out.reshape(populations.shape)


def solution(mesh):
    placed = (
        P("mode", None, "cell", None),
        P(None, "cell", None),
        P("mode"),
        P(None, "mode"),
        P("mode", None),
    )
    return jax.shard_map(
        on_device,
        mesh=mesh,
        in_specs=placed,
        out_specs=P("mode", None, "cell", None),
        check_vma=False,
    )
```

```python
import functools

import jax
import jax.numpy as jnp
from jax import lax
from jax.experimental import pallas as pl
from jax.experimental.pallas import tpu as pltpu
from jax.sharding import PartitionSpec as P

F32 = jnp.float32
BF16 = jnp.bfloat16
VMEM = pl.BlockSpec(memory_space=pltpu.VMEM)
HBM = pl.BlockSpec(memory_space=pltpu.HBM)


def call(body, outs, args, in_specs=None, out_specs=None, scratch=(), flops=0):
    total = sum(a.size * a.dtype.itemsize for a in (*outs, *args))
    if in_specs:
        args = [pltpu.with_memory_space_constraint(a, pltpu.HBM) if s is HBM else a for a, s in zip(args, in_specs)]
    return pl.pallas_call(
        body,
        out_shape=outs,
        in_specs=in_specs or [VMEM] * len(args),
        out_specs=out_specs or [VMEM] * len(outs),
        scratch_shapes=list(scratch),
        compiler_params=pltpu.CompilerParams(vmem_limit_bytes=24 * 2**20),
        cost_estimate=pl.CostEstimate(flops=flops, bytes_accessed=total, transcendentals=0),
    )(*args)


def shape(dims, dtype):
    return jax.ShapeDtypeStruct(dims, dtype)


def is_first():
    return 1 - lax.axis_index("cell") % 2


def source_row(r, rows):
    return r + is_first() * (rows - 1 - 2 * r)


def prepare(rows, pop_hbm, mask_hbm, octant_hbm, courant_hbm, *refs):
    q_refs, (p0_ref, keep_ref, coef_ref) = refs[:rows], refs[rows : rows + 3]
    pop_ref, mask_ref, octant_ref, courant_ref, sems = refs[rows + 3 :]
    pairs = (mask_hbm, mask_ref), (pop_hbm, pop_ref), (octant_hbm, octant_ref), (courant_hbm, courant_ref)
    copies = [pltpu.make_async_copy(*pair, sems.at[i]) for i, pair in enumerate(pairs)]
    for copy in copies:
        copy.start()
    modes = p0_ref.shape[1]
    copies[0].wait()
    copies[1].wait()
    for r in range(rows):
        source = source_row(r, rows)
        keep = (1 - mask_ref[pl.ds(source, 1), :]).astype(F32)
        row = keep * pop_ref[pl.ds(source, modes, stride=rows), :]
        keep_ref[r : r + 1, :] = keep
        p0_ref[r] = row
        q_refs[r][...] = row.astype(BF16)
    copies[2].wait()
    copies[3].wait()
    octant = octant_ref[...]
    speeds = [(1.0 - 2.0 * ((octant >> d) & 1).astype(F32)) * courant_ref[d : d + 1] for d in range(3)]
    flags = [(v < 0).astype(F32) for v in speeds]
    table = jnp.concatenate([jnp.abs(v) for v in speeds] + flags + flags[:2], axis=0)
    coef_ref[...] = table.T


def columns(offset, modes):
    position = lax.axis_index("mode") ^ offset
    return pl.ds(pl.multiple_of(position * modes, modes), modes)


def product(c_ref, offset, blocks):
    cols = columns(offset, blocks[0].shape[0])
    return jnp.dot(c_ref[:, cols], jnp.concatenate(blocks, axis=1), preferred_element_type=F32)


def backward_y(coef_ref):
    return (coef_ref[:, 4:5] > 0) == (is_first() == 0)


def near_terms(fields, q_refs, early, blocks, coef_ref, c_ref):
    rows = len(fields)
    modes, width = fields[0].shape
    ax, ay, az = (coef_ref[:, d : d + 1] for d in range(3))
    neg_x = coef_ref[:, 3:4] > 0
    after = backward_y(coef_ref)
    stay = 1.0 - (ax + ay + az)
    results = []
    for r, p in enumerate(fields):
        beside = jnp.where(neg_x, pltpu.roll(p, width - 1, 1), pltpu.roll(p, 1, 1))
        prior = fields[r - 1] if r > 0 else jnp.zeros_like(p)
        later = fields[r + 1] if r < rows - 1 else jnp.zeros_like(p)
        results.append(stay * p + ax * beside + ay * jnp.where(after, later, prior))
    total = product(c_ref, 0, [q[...] for q in q_refs])
    for i, offset in enumerate(early):
        total = total + product(c_ref, offset, [b[...] for b in blocks[i * rows : (i + 1) * rows]])
    return [v - total[:, r * width : (r + 1) * width] for r, v in enumerate(results)]


def far_terms(rows, late, blocks, inner, outer, coef_ref, c_ref):
    width = inner.shape[1]
    ay = coef_ref[:, 1:2]
    after = backward_y(coef_ref)
    results = [None] * rows
    if late:
        total = sum(
            product(c_ref, offset, [b[...] for b in blocks[i * rows : (i + 1) * rows]]) for i, offset in enumerate(late)
        )
        results = [-total[:, r * width : (r + 1) * width] for r in range(rows)]
    else:
        results = [jnp.zeros(inner.shape, F32)] * rows
    results[0] = results[0] + jnp.where(after, 0.0, ay * inner[...].astype(F32))
    results[-1] = results[-1] + jnp.where(after, ay * outer[...].astype(F32), 0.0)
    return results


def first_near(rows, early, *refs):
    p0_ref, coef_ref, c_hbm, *rest = refs
    q_refs, blocks = rest[:rows], rest[rows : rows * (1 + len(early))]
    base_ref, c_ref, sem = rest[rows * (1 + len(early)) :]
    copy = pltpu.make_async_copy(c_hbm, c_ref, sem)
    copy.start()
    copy.wait()
    for r, value in enumerate(near_terms([p0_ref[r] for r in range(rows)], q_refs, early, blocks, coef_ref, c_ref)):
        base_ref[r] = value


def first_end(rows, late, *refs):
    base_ref, keep_ref, coef_ref, c_ref, inner, outer, *rest = refs
    blocks, (*q_refs, p1_ref) = rest[: rows * len(late)], rest[rows * len(late) :]
    for r, term in enumerate(far_terms(rows, late, blocks, inner, outer, coef_ref, c_ref)):
        value = keep_ref[r : r + 1] * (base_ref[r] + term)
        p1_ref[r] = value
        q_refs[r][...] = value.astype(BF16)


def second_near(rows, early, *refs):
    p0_ref, p1_ref, coef_ref, c_ref, *rest = refs
    q_refs, blocks, base_ref = rest[:rows], rest[rows:-1], rest[-1]
    for r, value in enumerate(near_terms([p1_ref[r] for r in range(rows)], q_refs, early, blocks, coef_ref, c_ref)):
        base_ref[r] = 0.5 * p0_ref[r] + 0.5 * value


def second_end(rows, late, *refs):
    base_ref, keep_ref, coef_ref, c_ref, inner, outer, *rest = refs
    blocks, out_ref = rest[:-1], rest[-1]
    modes = out_ref.shape[0] // rows
    for r, term in enumerate(far_terms(rows, late, blocks, inner, outer, coef_ref, c_ref)):
        out_ref[pl.ds(source_row(r, rows), modes, stride=rows), :] = keep_ref[r : r + 1] * (base_ref[r] + 0.5 * term)


def later(row, other):
    def body(row_ref, _, out_ref):
        out_ref[...] = row_ref[...]

    (copied,) = call(body, [shape(row.shape, row.dtype)], [row, other], in_specs=[VMEM, pl.BlockSpec(memory_space=pl.ANY)])
    return copied


def exchange(q, count):
    bits = [1 << b for b in range(count.bit_length() - 1)]
    gathered = [{0: row} for row in q]
    orders = [bits if r % 2 == 0 else bits[::-1] for r in range(len(q))]
    for step in range(len(bits)):
        for held, order in zip(gathered, orders):
            bit = order[step]
            pairs = [(i, i ^ bit) for i in range(count)]
            held |= {o ^ bit: lax.ppermute(b, "mode", pairs) for o, b in held.items()}
    return gathered


def halo(q, block):
    count = lax.axis_size("cell")
    within = [(i, i ^ 1) for i in range(count)]
    between = [(i, i + 1) for i in range(1, count - 1, 2)]
    between += [(target, source) for source, target in between]
    return lax.ppermute(later(q[0], block), "cell", within), lax.ppermute(q[-1], "cell", between)


def on_device(populations, contact_mask, octant, courant, collision):
    modes, planes, rows, width = populations.shape
    count = lax.axis_size("mode")
    assert planes == 1 and lax.axis_size("cell") % 2 == 0 and count & (count - 1) == 0
    early = [1 << b for b in range(count.bit_length() - 1)]
    late = [o for o in range(1, count) if o not in early]
    pop = populations.reshape(modes * rows, width)
    mask = contact_mask.reshape(rows, width)
    octant = octant.reshape(1, modes)
    row_bf16 = shape((modes, width), BF16)
    all_rows = shape((rows, modes, width), F32)
    flops = 2 * modes * modes * rows * width
    near = flops * (1 + len(early))
    far = flops * len(late)

    *q, p0, keep, coef = call(
        functools.partial(prepare, rows),
        [row_bf16] * rows + [all_rows, shape((rows, width), F32), shape((modes, 8), F32)],
        [pop, mask, octant, courant],
        in_specs=[HBM] * 4,
        scratch=[pltpu.VMEM(a.shape, a.dtype) for a in (pop, mask, octant, courant)] + [pltpu.SemaphoreType.DMA((4,))],
    )
    gathered = exchange(q, count)
    inner, outer = halo(q, gathered[-1][early[0]])
    args = [p0, coef, collision, *q, *(g[o] for o in early for g in gathered)]
    base, c = call(
        functools.partial(first_near, rows, early),
        [all_rows, shape(collision.shape, collision.dtype)],
        args,
        in_specs=[VMEM, VMEM, HBM] + [VMEM] * (len(args) - 3),
        scratch=[pltpu.SemaphoreType.DMA],
        flops=near,
    )
    *q, p1 = call(
        functools.partial(first_end, rows, late),
        [row_bf16] * rows + [all_rows],
        [base, keep, coef, c, inner, outer, *(g[o] for o in late for g in gathered)],
        flops=far,
    )
    gathered = exchange(q, count)
    inner, outer = halo(q, gathered[-1][early[0]])
    (base,) = call(
        functools.partial(second_near, rows, early),
        [all_rows],
        [p0, p1, coef, c, *q, *(g[o] for o in early for g in gathered)],
        flops=near,
    )
    (out,) = call(
        functools.partial(second_end, rows, late),
        [shape((modes * rows, width), F32)],
        [base, keep, coef, c, inner, outer, *(g[o] for o in late for g in gathered)],
        flops=far,
    )
    return out.reshape(populations.shape)


def solution(mesh):
    placed = (
        P("mode", None, "cell", None),
        P(None, "cell", None),
        P("mode"),
        P(None, "mode"),
        P("mode", None),
    )
    return jax.shard_map(
        on_device,
        mesh=mesh,
        in_specs=placed,
        out_specs=P("mode", None, "cell", None),
        check_vma=False,
    )
```

```python
import functools

import jax
import jax.numpy as jnp
from jax import lax
from jax.experimental import pallas as pl
from jax.experimental.pallas import tpu as pltpu
from jax.sharding import PartitionSpec as P

F32 = jnp.float32
BF16 = jnp.bfloat16
VMEM = pl.BlockSpec(memory_space=pltpu.VMEM)
HBM = pl.BlockSpec(memory_space=pltpu.HBM)


def call(body, outs, args, in_specs=None, out_specs=None, scratch=(), flops=0):
    total = sum(a.size * a.dtype.itemsize for a in (*outs, *args))
    if in_specs:
        args = [pltpu.with_memory_space_constraint(a, pltpu.HBM) if s is HBM else a for a, s in zip(args, in_specs)]
    return pl.pallas_call(
        body,
        out_shape=outs,
        in_specs=in_specs or [VMEM] * len(args),
        out_specs=out_specs or [VMEM] * len(outs),
        scratch_shapes=list(scratch),
        compiler_params=pltpu.CompilerParams(vmem_limit_bytes=24 * 2**20),
        cost_estimate=pl.CostEstimate(flops=flops, bytes_accessed=total, transcendentals=0),
    )(*args)


def shape(dims, dtype):
    return jax.ShapeDtypeStruct(dims, dtype)


def is_first():
    return 1 - lax.axis_index("cell") % 2


def source_row(r, rows):
    return r + is_first() * (rows - 1 - 2 * r)


def prepare(rows, pop_hbm, mask_hbm, octant_hbm, courant_hbm, c_hbm, *refs):
    q_refs, (p0_ref, keep_ref, coef_ref, c_ref) = refs[:rows], refs[rows : rows + 4]
    pop_ref, mask_ref, octant_ref, courant_ref, sems = refs[rows + 4 :]
    pairs = (mask_hbm, mask_ref), (pop_hbm, pop_ref), (octant_hbm, octant_ref), (courant_hbm, courant_ref), (c_hbm, c_ref)
    copies = [pltpu.make_async_copy(*pair, sems.at[i]) for i, pair in enumerate(pairs)]
    for copy in copies:
        copy.start()
    modes = p0_ref.shape[1]
    copies[0].wait()
    copies[1].wait()
    for r in range(rows):
        source = source_row(r, rows)
        keep = (1 - mask_ref[pl.ds(source, 1), :]).astype(F32)
        row = keep * pop_ref[pl.ds(source, modes, stride=rows), :]
        keep_ref[r : r + 1, :] = keep
        p0_ref[r] = row
        q_refs[r][...] = row.astype(BF16)
    copies[2].wait()
    copies[3].wait()
    octant = octant_ref[...]
    speeds = [(1.0 - 2.0 * ((octant >> d) & 1).astype(F32)) * courant_ref[d : d + 1] for d in range(3)]
    flags = [(v < 0).astype(F32) for v in speeds]
    table = jnp.concatenate([jnp.abs(v) for v in speeds] + flags + flags[:2], axis=0)
    coef_ref[...] = table.T
    copies[4].wait()


def columns(offset, modes):
    position = lax.axis_index("mode") ^ offset
    return pl.ds(pl.multiple_of(position * modes, modes), modes)


def product(c_ref, offset, blocks):
    cols = columns(offset, blocks[0].shape[0])
    return jnp.dot(c_ref[:, cols], jnp.concatenate(blocks, axis=1), preferred_element_type=F32)


def backward_y(coef_ref):
    return (coef_ref[:, 4:5] > 0) == (is_first() == 0)


def drift(fields, coef_ref):
    rows = len(fields)
    width = fields[0].shape[1]
    ax, ay, az = (coef_ref[:, d : d + 1] for d in range(3))
    neg_x = coef_ref[:, 3:4] > 0
    after = backward_y(coef_ref)
    stay = 1.0 - (ax + ay + az)
    results = []
    for r, p in enumerate(fields):
        beside = jnp.where(neg_x, pltpu.roll(p, width - 1, 1), pltpu.roll(p, 1, 1))
        prior = fields[r - 1] if r > 0 else jnp.zeros_like(p)
        later = fields[r + 1] if r < rows - 1 else jnp.zeros_like(p)
        results.append(stay * p + ax * beside + ay * jnp.where(after, later, prior))
    return results


def near_products(q_refs, early, blocks, c_ref):
    rows = len(q_refs)
    total = product(c_ref, 0, [q[...] for q in q_refs])
    for i, offset in enumerate(early):
        total = total + product(c_ref, offset, [b[...] for b in blocks[i * rows : (i + 1) * rows]])
    width = total.shape[1] // rows
    return [total[:, r * width : (r + 1) * width] for r in range(rows)]


def far_terms(group, rows, late, refs, coef_ref, c_ref):
    ay = coef_ref[:, 1:2]
    after = backward_y(coef_ref)
    refs = list(refs)
    inner = refs.pop(0) if 0 in group else None
    outer = refs.pop(0) if rows - 1 in group else None
    count = len(group)
    blocks = [[b[...] for b in refs[i * count : (i + 1) * count]] for i in range(len(late))]
    total = sum(product(c_ref, offset, block) for offset, block in zip(late, blocks))
    results = []
    for i, r in enumerate(group):
        width = c_ref.shape[1] if not late else total.shape[1] // count
        value = -total[:, i * width : (i + 1) * width] if late else 0.0
        if r == 0:
            value = value + jnp.where(after, 0.0, ay * inner[...].astype(F32))
        if r == rows - 1:
            value = value + jnp.where(after, ay * outer[...].astype(F32), 0.0)
        results.append(value)
    return results


def first_near(rows, early, *refs):
    p0_ref, coef_ref, c_ref, *rest = refs
    q_refs, blocks, base_ref = rest[:rows], rest[rows:-1], rest[-1]
    moved = drift([p0_ref[r] for r in range(rows)], coef_ref)
    for r, value in enumerate(near_products(q_refs, early, blocks, c_ref)):
        base_ref[r] = moved[r] - value


def first_end(group, rows, late, *refs):
    base_ref, keep_ref, coef_ref, c_ref, *rest = refs
    inputs, outputs = rest[: -2 * len(group)], rest[-2 * len(group) :]
    for i, (r, term) in enumerate(zip(group, far_terms(group, rows, late, inputs, coef_ref, c_ref))):
        value = keep_ref[r : r + 1] * (base_ref[r] + term)
        outputs[2 * i][...] = value.astype(BF16)
        outputs[2 * i + 1][...] = value


def second_near(rows, early, *refs):
    p0_ref, coef_ref, c_ref, *rest = refs
    p1_refs, q_refs, blocks, base_ref = rest[:rows], rest[rows : 2 * rows], rest[2 * rows : -1], rest[-1]
    moved = drift([p[...] for p in p1_refs], coef_ref)
    for r, value in enumerate(near_products(q_refs, early, blocks, c_ref)):
        base_ref[r] = 0.5 * p0_ref[r] + 0.5 * (moved[r] - value)


def second_end(rows, late, *refs):
    base_ref, keep_ref, coef_ref, c_ref, *inputs, out_ref = refs
    modes = out_ref.shape[0] // rows
    for r, term in enumerate(far_terms(range(rows), rows, late, inputs, coef_ref, c_ref)):
        out_ref[pl.ds(source_row(r, rows), modes, stride=rows), :] = keep_ref[r : r + 1] * (base_ref[r] + 0.5 * term)


def later(row, other):
    def body(row_ref, _, out_ref):
        out_ref[...] = row_ref[...]

    (copied,) = call(body, [shape(row.shape, row.dtype)], [row, other], in_specs=[VMEM, pl.BlockSpec(memory_space=pl.ANY)])
    return copied


def exchange(row, r, count):
    bits = [1 << b for b in range(count.bit_length() - 1)]
    held = {0: row}
    for bit in bits if r % 2 == 0 else bits[::-1]:
        pairs = [(i, i ^ bit) for i in range(count)]
        held |= {o ^ bit: lax.ppermute(b, "mode", pairs) for o, b in held.items()}
    return held


def within_pair(row):
    return lax.ppermute(row, "cell", [(i, i ^ 1) for i in range(lax.axis_size("cell"))])


def between_pairs(row):
    steps = [(i, i + 1) for i in range(1, lax.axis_size("cell") - 1, 2)]
    return lax.ppermute(row, "cell", steps + [(target, source) for source, target in steps])


def on_device(populations, contact_mask, octant, courant, collision):
    modes, planes, rows, width = populations.shape
    count = lax.axis_size("mode")
    assert planes == 1 and lax.axis_size("cell") % 2 == 0 and count & (count - 1) == 0
    early = [1 << b for b in range(count.bit_length() - 1)]
    late = [o for o in range(1, count) if o not in early]
    pop = populations.reshape(modes * rows, width)
    mask = contact_mask.reshape(rows, width)
    octant = octant.reshape(1, modes)
    row_bf16 = shape((modes, width), BF16)
    all_rows = shape((rows, modes, width), F32)
    flops = 2 * modes * modes * rows * width
    near = flops * (1 + len(early))
    far = flops * len(late)

    *q, p0, keep, coef, c = call(
        functools.partial(prepare, rows),
        [row_bf16] * rows + [all_rows, shape((rows, width), F32), shape((modes, 8), F32), shape(collision.shape, BF16)],
        [pop, mask, octant, courant, collision],
        in_specs=[HBM] * 5,
        scratch=[pltpu.VMEM(a.shape, a.dtype) for a in (pop, mask, octant, courant)] + [pltpu.SemaphoreType.DMA((5,))],
    )
    last = rows - 1
    groups = [g for g in (range(last), range(last, rows)) if len(g)]
    inner = within_pair(q[0])
    gathered = [exchange(row, r, count) for r, row in enumerate(q)]
    outer = between_pairs(later(q[last], inner))
    (base,) = call(
        functools.partial(first_near, rows, early),
        [all_rows],
        [p0, coef, c, *q, *(g[o] for o in early for g in gathered)],
        flops=near,
    )
    q, p1, held = [], [], []
    for group in groups:
        halo = [inner] * (0 in group) + [outer] * (last in group)
        results = call(
            functools.partial(first_end, group, rows, late),
            [row_bf16, shape((modes, width), F32)] * len(group),
            [base, keep, coef, c, *halo, *(gathered[r][o] for o in late for r in group)],
            flops=far,
        )
        q += results[::2]
        p1 += results[1::2]
        if 0 in group:
            second_inner = within_pair(q[0])
        held += [exchange(q[r], r, count) for r in group]
    inner, gathered = second_inner, held
    outer = between_pairs(later(q[last], inner))
    (base,) = call(
        functools.partial(second_near, rows, early),
        [all_rows],
        [p0, coef, c, *p1, *q, *(g[o] for o in early for g in gathered)],
        flops=near,
    )
    (out,) = call(
        functools.partial(second_end, rows, late),
        [shape((modes * rows, width), F32)],
        [base, keep, coef, c, inner, outer, *(g[o] for o in late for g in gathered)],
        flops=far,
    )
    return out.reshape(populations.shape)


def solution(mesh):
    placed = (
        P("mode", None, "cell", None),
        P(None, "cell", None),
        P("mode"),
        P(None, "mode"),
        P("mode", None),
    )
    return jax.shard_map(
        on_device,
        mesh=mesh,
        in_specs=placed,
        out_specs=P("mode", None, "cell", None),
        check_vma=False,
    )
```

```python
import functools

import jax
import jax.numpy as jnp
from jax import lax
from jax.experimental import pallas as pl
from jax.experimental.pallas import tpu as pltpu
from jax.sharding import PartitionSpec as P

F32 = jnp.float32
BF16 = jnp.bfloat16
ANY = pl.BlockSpec(memory_space=pl.ANY)
HBM = pl.BlockSpec(memory_space=pltpu.HBM)
VMEM = pl.BlockSpec(memory_space=pltpu.VMEM)


def shape(dims, dtype):
    return jax.ShapeDtypeStruct(dims, dtype)


def call(body, ins, outs, hbm=(), after=(), scratch=(), flops=0):
    names, out_names = list(ins), list(outs)
    args = [pltpu.with_memory_space_constraint(ins[n], pltpu.HBM) if n in hbm else ins[n] for n in names]
    args += list(after)
    total = sum(a.size * a.dtype.itemsize for a in (*outs.values(), *args))

    def kernel(*refs):
        a, b = len(args), len(args) + len(outs)
        body(dict(zip(names, refs)), dict(zip(out_names, refs[a:b])), *refs[b:])

    results = pl.pallas_call(
        kernel,
        out_shape=list(outs.values()),
        in_specs=[HBM if n in hbm else VMEM for n in names] + [ANY] * len(after),
        out_specs=[VMEM] * len(outs),
        scratch_shapes=list(scratch),
        compiler_params=pltpu.CompilerParams(vmem_limit_bytes=24 * 2**20),
        cost_estimate=pl.CostEstimate(flops=flops, bytes_accessed=total, transcendentals=0),
    )(*args)
    return dict(zip(out_names, results))


def is_first():
    return 1 - lax.axis_index("cell") % 2


def source_row(r, rows):
    return r + is_first() * (rows - 1 - 2 * r)


def prepare(rows, ins, outs, pop, mask, sems):
    copies = [
        pltpu.make_async_copy(ins["mask"], mask, sems.at[0]),
        pltpu.make_async_copy(ins["pop"], pop, sems.at[1]),
    ]
    for copy in copies:
        copy.start()
    for copy in copies:
        copy.wait()
    modes = outs["p0"].shape[0]
    for r in range(rows):
        source = source_row(r, rows)
        keep = (1 - mask[pl.ds(source, 1), :]).astype(F32)
        row = keep * pop[pl.ds(source, modes, stride=rows), :]
        outs["keep"][r : r + 1, :] = keep
        outs[f"p{r}"][...] = row
        outs[f"q{r}"][...] = row.astype(BF16)


def coefficients(octant, courant):
    speeds = [(1.0 - 2.0 * ((octant >> d) & 1).astype(F32)) * courant[d : d + 1] for d in range(3)]
    flags = [(v < 0).astype(F32) for v in speeds]
    return jnp.concatenate([jnp.abs(v) for v in speeds] + flags + flags[:2], axis=0).T


def backward_y(coef):
    return (coef[:, 4:5] > 0) == (is_first() == 0)


def drift(fields, r, coef):
    p = fields[r]
    width = p.shape[1]
    ax, ay, az = (coef[:, d : d + 1] for d in range(3))
    beside = jnp.where(coef[:, 3:4] > 0, pltpu.roll(p, width - 1, 1), pltpu.roll(p, 1, 1))
    prior = fields[r - 1] if r > 0 else jnp.zeros_like(p)
    later = fields[r + 1] if r < len(fields) - 1 else jnp.zeros_like(p)
    return (1.0 - (ax + ay + az)) * p + ax * beside + ay * jnp.where(backward_y(coef), later, prior)


def product(c, offset, blocks):
    modes = blocks[0].shape[0]
    position = lax.axis_index("mode") ^ offset
    cols = pl.ds(pl.multiple_of(position * modes, modes), modes)
    return jnp.dot(c[:, cols], jnp.concatenate(blocks, axis=1), preferred_element_type=F32)


def begin(rows, ins, outs, octant, courant, sems):
    copies = [
        pltpu.make_async_copy(ins["octant"], octant, sems.at[0]),
        pltpu.make_async_copy(ins["courant"], courant, sems.at[1]),
        pltpu.make_async_copy(ins["collision"], outs["c"], sems.at[2]),
    ]
    for copy in copies:
        copy.start()
    copies[0].wait()
    copies[1].wait()
    coef = coefficients(octant[...], courant[...])
    outs["coef"][...] = coef
    fields = [ins[f"p{r}"][...] for r in range(rows)]
    for r in range(rows):
        outs[f"sum{r}"][...] = drift(fields, r, coef)
    copies[2].wait()


def step(rows, which, moves, keys, halos, ends, second, ins, outs):
    values = {r: 0.0 if moves else ins[f"sum{r}"][...] for r in which}
    if moves:
        fields = [ins[f"p{r}"][...] for r in range(rows)]
        values = {r: drift(fields, r, ins["coef"]) for r in which}
    if "inner" in halos:
        values[0] += jnp.where(backward_y(ins["coef"]), 0.0, ins["coef"][:, 1:2] * ins["inner"][...].astype(F32))
    if "outer" in halos:
        values[rows - 1] += jnp.where(backward_y(ins["coef"]), ins["coef"][:, 1:2] * ins["outer"][...].astype(F32), 0.0)
    for offset in sorted({o for o, _ in keys}):
        having = [r for r in which if (offset, r) in keys]
        result = product(ins["c"], offset, [ins[f"b{offset}_{r}"][...] for r in having])
        width = result.shape[1] // len(having)
        for i, r in enumerate(having):
            values[r] = values[r] - result[:, i * width : (i + 1) * width]
    for r, value in values.items():
        if not ends:
            outs[f"sum{r}"][...] = value
        elif not second:
            value = ins["keep"][r : r + 1] * value
            outs[f"p{r}"][...] = value
            outs[f"q{r}"][...] = value.astype(BF16)
        else:
            modes = outs["out"].shape[0] // rows
            value = ins["keep"][r : r + 1] * (0.5 * ins[f"first{r}"][...] + 0.5 * value)
            outs["out"][pl.ds(source_row(r, rows), modes, stride=rows), :] = value


def held(row, other):
    def body(ins, outs):
        outs["row"][...] = ins["row"][...]

    return call(body, {"row": row}, {"row": shape(row.shape, row.dtype)}, after=[other])["row"]


def exchange(row, bits, count, other=None):
    blocks = {0: row}
    for i, bit in enumerate(bits):
        pairs = [(j, j ^ bit) for j in range(count)]
        for offset, block in list(blocks.items()):
            if i and offset and other is not None:
                block = held(block, other)
            blocks[offset ^ bit] = lax.ppermute(block, "mode", pairs)
    return blocks


def within_pair(row):
    return lax.ppermute(row, "cell", [(i, i ^ 1) for i in range(lax.axis_size("cell"))])


def between_pairs(row):
    steps = [(i, i + 1) for i in range(1, lax.axis_size("cell") - 1, 2)]
    return lax.ppermute(row, "cell", steps + [(target, source) for source, target in steps])


def on_device(populations, contact_mask, octant, courant, collision):
    modes, planes, rows, width = populations.shape
    count = lax.axis_size("mode")
    assert planes == 1 and lax.axis_size("cell") % 2 == 0 and count & (count - 1) == 0
    last = rows - 1
    bits = [1 << b for b in range(count.bit_length() - 1)]
    orders = [bits if r % 2 == 0 else bits[::-1] for r in range(rows)]
    row_f32, row_bf16 = shape((modes, width), F32), shape((modes, width), BF16)
    keys = [(o, r) for r in range(rows) for o in range(count)]
    near = [(o, r) for o, r in keys if o == 0 or o in bits]
    far = [key for key in keys if key not in near]

    pop, mask = populations.reshape(modes * rows, width), contact_mask.reshape(rows, width)
    outs = {"keep": shape((rows, width), F32)}
    for r in range(rows):
        outs |= {f"p{r}": row_f32, f"q{r}": row_bf16}
    env = call(
        functools.partial(prepare, rows),
        {"pop": pop, "mask": mask},
        outs,
        hbm=("pop", "mask"),
        scratch=[pltpu.VMEM(pop.shape, F32), pltpu.VMEM(mask.shape, jnp.int32), pltpu.SemaphoreType.DMA((2,))],
    )
    first = {f"first{r}": env[f"p{r}"] for r in range(rows)}

    def run(blocks, which, moves, keys, halos, ends, second):
        names = [f"p{r}" for r in range(rows)] if moves else [f"sum{r}" for r in which]
        names += [*halos] + ["coef"] * (moves or len(halos) > 0) + ["c"] * (len(keys) > 0) + ["keep"] * ends
        ins = {n: env[n] for n in names} | {f"b{o}_{r}": blocks[r][o] for o, r in keys}
        if not ends:
            outs = {f"sum{r}": row_f32 for r in which}
        elif not second:
            outs = {f"p{r}": row_f32 for r in which} | {f"q{r}": row_bf16 for r in which}
        else:
            ins |= first
            outs = {"out": shape((modes * rows, width), F32)}
        body = functools.partial(step, rows, which, moves, keys, halos, ends, second)
        env.update(call(body, ins, outs, flops=2 * modes * modes * width * len(keys)))

    env["inner"] = within_pair(env["q0"])
    env |= call(
        functools.partial(begin, rows),
        {"octant": octant.reshape(1, modes), "courant": courant, "collision": collision}
        | {f"p{r}": env[f"p{r}"] for r in range(rows)},
        {"c": shape(collision.shape, BF16), "coef": shape((modes, 8), F32)} | {f"sum{r}": row_f32 for r in range(rows)},
        hbm=("octant", "courant", "collision"),
        scratch=[pltpu.VMEM((1, modes), jnp.int32), pltpu.VMEM(courant.shape, F32), pltpu.SemaphoreType.DMA((3,))],
    )
    blocks = [exchange(env[f"q{r}"], orders[r], count, env["c"] if r == 0 else None) for r in range(rows)]
    env["outer"] = between_pairs(held(env[f"q{last}"], env["inner"]))
    run(blocks, range(rows), False, near, ["inner"], False, False)
    if last:
        run(blocks, range(last), False, [k for k in far if k[1] < last], [], True, False)
    run(blocks, range(last, rows), False, [k for k in far if k[1] == last], [], False, False)
    run(blocks, range(last, rows), False, [], ["outer"], True, False)

    env["inner"] = within_pair(env["q0"])
    blocks = [exchange(env[f"q{r}"], orders[r], count) for r in range(rows)]
    env["outer"] = between_pairs(held(env[f"q{last}"], env["inner"]))
    run(blocks, range(rows), True, near, ["inner"], False, True)
    run(blocks, range(rows), False, far, ["outer"], True, True)
    return env["out"].reshape(populations.shape)


def solution(mesh):
    placed = (
        P("mode", None, "cell", None),
        P(None, "cell", None),
        P("mode"),
        P(None, "mode"),
        P("mode", None),
    )
    return jax.shard_map(
        on_device,
        mesh=mesh,
        in_specs=placed,
        out_specs=P("mode", None, "cell", None),
        check_vma=False,
    )
```

```python
import functools

import jax
import jax.numpy as jnp
from jax import lax
from jax.experimental import pallas as pl
from jax.experimental.pallas import tpu as pltpu
from jax.sharding import PartitionSpec as P

F32 = jnp.float32
BF16 = jnp.bfloat16
ANY = pl.BlockSpec(memory_space=pl.ANY)
HBM = pl.BlockSpec(memory_space=pltpu.HBM)
VMEM = pl.BlockSpec(memory_space=pltpu.VMEM)


def shape(dims, dtype):
    return jax.ShapeDtypeStruct(dims, dtype)


def call(body, ins, outs, hbm=(), after=(), scratch=(), flops=0):
    names, out_names = list(ins), list(outs)
    args = [pltpu.with_memory_space_constraint(ins[n], pltpu.HBM) if n in hbm else ins[n] for n in names]
    args += list(after)
    total = sum(a.size * a.dtype.itemsize for a in (*outs.values(), *args))

    def kernel(*refs):
        a, b = len(args), len(args) + len(outs)
        body(dict(zip(names, refs)), dict(zip(out_names, refs[a:b])), *refs[b:])

    results = pl.pallas_call(
        kernel,
        out_shape=list(outs.values()),
        in_specs=[HBM if n in hbm else VMEM for n in names] + [ANY] * len(after),
        out_specs=[VMEM] * len(outs),
        scratch_shapes=list(scratch),
        compiler_params=pltpu.CompilerParams(vmem_limit_bytes=24 * 2**20),
        cost_estimate=pl.CostEstimate(flops=flops, bytes_accessed=total, transcendentals=0),
    )(*args)
    return dict(zip(out_names, results))


def is_first():
    return 1 - lax.axis_index("cell") % 2


def source_row(r, rows):
    return r + is_first() * (rows - 1 - 2 * r)


def prepare(rows, ins, outs, pop, mask, sems):
    copies = [
        pltpu.make_async_copy(ins["mask"], mask, sems.at[0]),
        pltpu.make_async_copy(ins["pop"], pop, sems.at[1]),
    ]
    for copy in copies:
        copy.start()
    for copy in copies:
        copy.wait()
    modes = outs["p0"].shape[0]
    for r in range(rows):
        source = source_row(r, rows)
        keep = (1 - mask[pl.ds(source, 1), :]).astype(F32)
        row = keep * pop[pl.ds(source, modes, stride=rows), :]
        outs["keep"][r : r + 1, :] = keep
        outs[f"p{r}"][...] = row
        outs[f"q{r}"][...] = row.astype(BF16)


def coefficients(octant, courant):
    speeds = [(1.0 - 2.0 * ((octant >> d) & 1).astype(F32)) * courant[d : d + 1] for d in range(3)]
    flags = [(v < 0).astype(F32) for v in speeds]
    return jnp.concatenate([jnp.abs(v) for v in speeds] + flags + flags[:2], axis=0).T


def backward_y(coef):
    return (coef[:, 4:5] > 0) == (is_first() == 0)


def drift(fields, r, coef):
    p = fields[r]
    width = p.shape[1]
    ax, ay, az = (coef[:, d : d + 1] for d in range(3))
    beside = jnp.where(coef[:, 3:4] > 0, pltpu.roll(p, width - 1, 1), pltpu.roll(p, 1, 1))
    prior = fields[r - 1] if r > 0 else jnp.zeros_like(p)
    later = fields[r + 1] if r < len(fields) - 1 else jnp.zeros_like(p)
    return (1.0 - (ax + ay + az)) * p + ax * beside + ay * jnp.where(backward_y(coef), later, prior)


def mirrored(offset, count):
    bits = count.bit_length() - 1
    return sum((offset >> b & 1) << (bits - 1 - b) for b in range(bits))


def product(c, offset, blocks):
    modes = blocks[0].shape[0]
    other = mirrored(offset, c.shape[1] // modes)
    position = lax.axis_index("mode") ^ (is_first() * offset + (1 - is_first()) * other)
    cols = pl.ds(pl.multiple_of(position * modes, modes), modes)
    return jnp.dot(c[:, cols], jnp.concatenate(blocks, axis=1), preferred_element_type=F32)


def begin(rows, ins, outs, octant, courant, sems):
    copies = [
        pltpu.make_async_copy(ins["octant"], octant, sems.at[0]),
        pltpu.make_async_copy(ins["courant"], courant, sems.at[1]),
        pltpu.make_async_copy(ins["collision"], outs["c"], sems.at[2]),
    ]
    for copy in copies:
        copy.start()
    copies[0].wait()
    copies[1].wait()
    coef = coefficients(octant[...], courant[...])
    outs["coef"][...] = coef
    fields = [ins[f"p{r}"][...] for r in range(rows)]
    for r in range(rows):
        outs[f"sum{r}"][...] = drift(fields, r, coef)
    copies[2].wait()


def step(rows, which, moves, keys, halos, ends, second, ins, outs):
    values = {r: 0.0 if moves else ins[f"sum{r}"][...] for r in which}
    if moves:
        fields = [ins[f"p{r}"][...] for r in range(rows)]
        values = {r: drift(fields, r, ins["coef"]) for r in which}
    if "inner" in halos:
        values[0] += jnp.where(backward_y(ins["coef"]), 0.0, ins["coef"][:, 1:2] * ins["inner"][...].astype(F32))
    if "outer" in halos:
        values[rows - 1] += jnp.where(backward_y(ins["coef"]), ins["coef"][:, 1:2] * ins["outer"][...].astype(F32), 0.0)
    for offset in sorted({o for o, _ in keys}):
        having = [r for r in which if (offset, r) in keys]
        result = product(ins["c"], offset, [ins[f"b{offset}_{r}"][...] for r in having])
        width = result.shape[1] // len(having)
        for i, r in enumerate(having):
            values[r] = values[r] - result[:, i * width : (i + 1) * width]
    for r, value in values.items():
        if not ends:
            outs[f"sum{r}"][...] = value
        elif not second:
            value = ins["keep"][r : r + 1] * value
            outs[f"p{r}"][...] = value
            outs[f"q{r}"][...] = value.astype(BF16)
        else:
            modes = outs["out"].shape[0] // rows
            value = ins["keep"][r : r + 1] * (0.5 * ins[f"first{r}"][...] + 0.5 * value)
            outs["out"][pl.ds(source_row(r, rows), modes, stride=rows), :] = value


def held(row, other):
    def body(ins, outs):
        outs["row"][...] = ins["row"][...]

    return call(body, {"row": row}, {"row": shape(row.shape, row.dtype)}, after=[other])["row"]


def exchange(row, bits, count, other=None):
    cells = lax.axis_size("cell")
    blocks = {0: row}
    for i, bit in enumerate(bits):
        both = bit, mirrored(bit, count)
        pairs = [(m * cells + c, (m ^ both[c % 2]) * cells + c) for m in range(count) for c in range(cells)]
        for offset, block in list(blocks.items()):
            if i and offset and other is not None:
                block = held(block, other)
            blocks[offset ^ bit] = lax.ppermute(block, ("mode", "cell"), pairs)
    return blocks


def within_pair(row):
    return lax.ppermute(row, "cell", [(i, i ^ 1) for i in range(lax.axis_size("cell"))])


def between_pairs(row):
    steps = [(i, i + 1) for i in range(1, lax.axis_size("cell") - 1, 2)]
    return lax.ppermute(row, "cell", steps + [(target, source) for source, target in steps])


def on_device(populations, contact_mask, octant, courant, collision):
    modes, planes, rows, width = populations.shape
    count = lax.axis_size("mode")
    assert planes == 1 and lax.axis_size("cell") % 2 == 0 and count & (count - 1) == 0
    last = rows - 1
    bits = [1 << b for b in range(count.bit_length() - 1)]
    orders = [bits if r % 2 == 0 else bits[::-1] for r in range(rows)]
    turned = [order[::-1] for order in orders]
    row_f32, row_bf16 = shape((modes, width), F32), shape((modes, width), BF16)
    keys = [(o, r) for r in range(rows) for o in range(count)]
    near = [(o, r) for o, r in keys if o == 0 or o in bits]
    far = [key for key in keys if key not in near]

    pop, mask = populations.reshape(modes * rows, width), contact_mask.reshape(rows, width)
    outs = {"keep": shape((rows, width), F32)}
    for r in range(rows):
        outs |= {f"p{r}": row_f32, f"q{r}": row_bf16}
    env = call(
        functools.partial(prepare, rows),
        {"pop": pop, "mask": mask},
        outs,
        hbm=("pop", "mask"),
        scratch=[pltpu.VMEM(pop.shape, F32), pltpu.VMEM(mask.shape, jnp.int32), pltpu.SemaphoreType.DMA((2,))],
    )
    first = {f"first{r}": env[f"p{r}"] for r in range(rows)}

    def run(blocks, which, moves, keys, halos, ends, second):
        names = [f"p{r}" for r in range(rows)] if moves else [f"sum{r}" for r in which]
        names += [*halos] + ["coef"] * (moves or len(halos) > 0) + ["c"] * (len(keys) > 0) + ["keep"] * ends
        ins = {n: env[n] for n in names} | {f"b{o}_{r}": blocks[r][o] for o, r in keys}
        if not ends:
            outs = {f"sum{r}": row_f32 for r in which}
        elif not second:
            outs = {f"p{r}": row_f32 for r in which} | {f"q{r}": row_bf16 for r in which}
        else:
            ins |= first
            outs = {"out": shape((modes * rows, width), F32)}
        body = functools.partial(step, rows, which, moves, keys, halos, ends, second)
        env.update(call(body, ins, outs, flops=2 * modes * modes * width * len(keys)))

    env["inner"] = within_pair(env["q0"])
    env |= call(
        functools.partial(begin, rows),
        {"octant": octant.reshape(1, modes), "courant": courant, "collision": collision}
        | {f"p{r}": env[f"p{r}"] for r in range(rows)},
        {"c": shape(collision.shape, BF16), "coef": shape((modes, 8), F32)} | {f"sum{r}": row_f32 for r in range(rows)},
        hbm=("octant", "courant", "collision"),
        scratch=[pltpu.VMEM((1, modes), jnp.int32), pltpu.VMEM(courant.shape, F32), pltpu.SemaphoreType.DMA((3,))],
    )
    blocks = [exchange(env[f"q{r}"], turned[r], count, env["c"] if r == 0 else None) for r in range(rows)]
    env["outer"] = between_pairs(held(env[f"q{last}"], env["inner"]))
    run(blocks, range(rows), False, near, ["inner"], False, False)
    if last:
        run(blocks, range(last), False, [k for k in far if k[1] < last], [], True, False)
    run(blocks, range(last, rows), False, [k for k in far if k[1] == last], ["outer"], True, False)

    env["inner"] = within_pair(env["q0"])
    blocks = [exchange(env[f"q{r}"], orders[r], count) for r in range(rows)]
    env["outer"] = between_pairs(held(env[f"q{last}"], env["inner"]))
    run(blocks, range(rows), True, near, ["inner"], False, True)
    run(blocks, range(rows), False, far, ["outer"], True, True)
    return env["out"].reshape(populations.shape)


def solution(mesh):
    placed = (
        P("mode", None, "cell", None),
        P(None, "cell", None),
        P("mode"),
        P(None, "mode"),
        P("mode", None),
    )
    return jax.shard_map(
        on_device,
        mesh=mesh,
        in_specs=placed,
        out_specs=P("mode", None, "cell", None),
        check_vma=False,
    )
```

```python
import functools

import jax
import jax.numpy as jnp
from jax import lax
from jax.experimental import pallas as pl
from jax.experimental.pallas import tpu as pltpu
from jax.sharding import PartitionSpec as P

F32 = jnp.float32
BF16 = jnp.bfloat16
ANY = pl.BlockSpec(memory_space=pl.ANY)
HBM = pl.BlockSpec(memory_space=pltpu.HBM)
VMEM = pl.BlockSpec(memory_space=pltpu.VMEM)


def shape(dims, dtype):
    return jax.ShapeDtypeStruct(dims, dtype)


def call(body, ins, outs, hbm=(), after=(), scratch=(), flops=0):
    names, out_names = list(ins), list(outs)
    args = [pltpu.with_memory_space_constraint(ins[n], pltpu.HBM) if n in hbm else ins[n] for n in names]
    args += list(after)
    total = sum(a.size * a.dtype.itemsize for a in (*outs.values(), *args))

    def kernel(*refs):
        a, b = len(args), len(args) + len(outs)
        body(dict(zip(names, refs)), dict(zip(out_names, refs[a:b])), *refs[b:])

    results = pl.pallas_call(
        kernel,
        out_shape=list(outs.values()),
        in_specs=[HBM if n in hbm else VMEM for n in names] + [ANY] * len(after),
        out_specs=[VMEM] * len(outs),
        scratch_shapes=list(scratch),
        compiler_params=pltpu.CompilerParams(vmem_limit_bytes=24 * 2**20),
        cost_estimate=pl.CostEstimate(flops=flops, bytes_accessed=total, transcendentals=0),
    )(*args)
    return dict(zip(out_names, results))


def is_first():
    return 1 - lax.axis_index("cell") % 2


def turned(values):
    first = is_first() == 1
    return [jnp.where(first, other, value) for value, other in zip(values, values[::-1])]


def prepare(rows, ins, outs, pop, mask, sems):
    copies = [
        pltpu.make_async_copy(ins["mask"], mask, sems.at[0]),
        pltpu.make_async_copy(ins["pop"], pop, sems.at[1]),
    ]
    for copy in copies:
        copy.start()
    for copy in copies:
        copy.wait()
    modes = outs["p0"].shape[0]
    keeps = turned([(1 - mask[r : r + 1, :]).astype(F32) for r in range(rows)])
    fields = turned([pop[pl.ds(r, modes, stride=rows), :] for r in range(rows)])
    for r, (keep, field) in enumerate(zip(keeps, fields)):
        row = keep * field
        outs["keep"][r : r + 1, :] = keep
        outs[f"p{r}"][...] = row
        outs[f"q{r}"][...] = row.astype(BF16)


def coefficients(octant, courant):
    speeds = [(1.0 - 2.0 * ((octant >> d) & 1).astype(F32)) * courant[d : d + 1] for d in range(3)]
    flags = [(v < 0).astype(F32) for v in speeds]
    return jnp.concatenate([jnp.abs(v) for v in speeds] + flags + flags[:2], axis=0).T


def backward_y(coef):
    return (coef[:, 4:5] > 0) == (is_first() == 0)


def drift(fields, r, coef):
    p = fields[r]
    width = p.shape[1]
    ax, ay, az = (coef[:, d : d + 1] for d in range(3))
    beside = jnp.where(coef[:, 3:4] > 0, pltpu.roll(p, width - 1, 1), pltpu.roll(p, 1, 1))
    prior = fields[r - 1] if r > 0 else jnp.zeros_like(p)
    later = fields[r + 1] if r < len(fields) - 1 else jnp.zeros_like(p)
    return (1.0 - (ax + ay + az)) * p + ax * beside + ay * jnp.where(backward_y(coef), later, prior)


def mirrored(offset, count):
    bits = count.bit_length() - 1
    return sum((offset >> b & 1) << (bits - 1 - b) for b in range(bits))


def product(c, offset, blocks):
    modes = blocks[0].shape[0]
    other = mirrored(offset, c.shape[1] // modes)
    position = lax.axis_index("mode") ^ (is_first() * offset + (1 - is_first()) * other)
    cols = pl.ds(pl.multiple_of(position * modes, modes), modes)
    return jnp.dot(c[:, cols], jnp.concatenate(blocks, axis=1), preferred_element_type=F32)


def begin(rows, ins, outs, octant, courant, sems):
    copies = [
        pltpu.make_async_copy(ins["octant"], octant, sems.at[0]),
        pltpu.make_async_copy(ins["courant"], courant, sems.at[1]),
        pltpu.make_async_copy(ins["collision"], outs["c"], sems.at[2]),
    ]
    for copy in copies:
        copy.start()
    copies[0].wait()
    copies[1].wait()
    coef = coefficients(octant[...], courant[...])
    outs["coef"][...] = coef
    fields = [ins[f"p{r}"][...] for r in range(rows)]
    for r in range(rows):
        outs[f"sum{r}"][...] = drift(fields, r, coef)
    copies[2].wait()


def step(rows, which, moves, keys, halos, ends, second, ins, outs):
    values = {r: 0.0 if moves else ins[f"sum{r}"][...] for r in which}
    if moves:
        fields = [ins[f"p{r}"][...] for r in range(rows)]
        values = {r: drift(fields, r, ins["coef"]) for r in which}
    if "inner" in halos:
        values[0] += jnp.where(backward_y(ins["coef"]), 0.0, ins["coef"][:, 1:2] * ins["inner"][...].astype(F32))
    if "outer" in halos:
        values[rows - 1] += jnp.where(backward_y(ins["coef"]), ins["coef"][:, 1:2] * ins["outer"][...].astype(F32), 0.0)
    for offset in sorted({o for o, _ in keys}):
        having = [r for r in which if (offset, r) in keys]
        result = product(ins["c"], offset, [ins[f"b{offset}_{r}"][...] for r in having])
        width = result.shape[1] // len(having)
        for i, r in enumerate(having):
            values[r] = values[r] - result[:, i * width : (i + 1) * width]
    if ends and second:
        modes = outs["out"].shape[0] // rows
        last = [ins["keep"][r : r + 1] * (0.5 * ins[f"first{r}"][...] + 0.5 * values[r]) for r in range(rows)]
        for r, value in enumerate(turned(last)):
            outs["out"][pl.ds(r, modes, stride=rows), :] = value
        return
    for r, value in values.items():
        if ends:
            value = ins["keep"][r : r + 1] * value
            outs[f"p{r}"][...] = value
            outs[f"q{r}"][...] = value.astype(BF16)
        else:
            outs[f"sum{r}"][...] = value


def held(row, other):
    def body(ins, outs):
        outs["row"][...] = ins["row"][...]

    return call(body, {"row": row}, {"row": shape(row.shape, row.dtype)}, after=[other])["row"]


def exchange(row, bits, count, other=None):
    cells = lax.axis_size("cell")
    blocks = {0: row}
    for i, bit in enumerate(bits):
        both = bit, mirrored(bit, count)
        pairs = [(m * cells + c, (m ^ both[c % 2]) * cells + c) for m in range(count) for c in range(cells)]
        for offset, block in list(blocks.items()):
            if i and offset and other is not None:
                block = held(block, other)
            blocks[offset ^ bit] = lax.ppermute(block, ("mode", "cell"), pairs)
    return blocks


def within_pair(row):
    return lax.ppermute(row, "cell", [(i, i ^ 1) for i in range(lax.axis_size("cell"))])


def between_pairs(row):
    steps = [(i, i + 1) for i in range(1, lax.axis_size("cell") - 1, 2)]
    return lax.ppermute(row, "cell", steps + [(target, source) for source, target in steps])


def on_device(populations, contact_mask, octant, courant, collision):
    modes, planes, rows, width = populations.shape
    count = lax.axis_size("mode")
    assert planes == 1 and lax.axis_size("cell") % 2 == 0 and count & (count - 1) == 0
    last = rows - 1
    bits = [1 << b for b in range(count.bit_length() - 1)]
    orders = [bits if r % 2 == 0 else bits[::-1] for r in range(rows)]
    row_f32, row_bf16 = shape((modes, width), F32), shape((modes, width), BF16)
    keys = [(o, r) for r in range(rows) for o in range(count)]
    near = [(o, r) for o, r in keys if o == 0 or o in bits]
    far = [key for key in keys if key not in near]

    pop, mask = populations.reshape(modes * rows, width), contact_mask.reshape(rows, width)
    outs = {"keep": shape((rows, width), F32)}
    for r in range(rows):
        outs |= {f"p{r}": row_f32, f"q{r}": row_bf16}
    env = call(
        functools.partial(prepare, rows),
        {"pop": pop, "mask": mask},
        outs,
        hbm=("pop", "mask"),
        scratch=[pltpu.VMEM(pop.shape, F32), pltpu.VMEM(mask.shape, jnp.int32), pltpu.SemaphoreType.DMA((2,))],
    )
    first = {f"first{r}": env[f"p{r}"] for r in range(rows)}

    def run(blocks, which, moves, keys, halos, ends, second):
        names = [f"p{r}" for r in range(rows)] if moves else [f"sum{r}" for r in which]
        names += [*halos] + ["coef"] * (moves or len(halos) > 0) + ["c"] * (len(keys) > 0) + ["keep"] * ends
        ins = {n: env[n] for n in names} | {f"b{o}_{r}": blocks[r][o] for o, r in keys}
        if not ends:
            outs = {f"sum{r}": row_f32 for r in which}
        elif not second:
            outs = {f"p{r}": row_f32 for r in which} | {f"q{r}": row_bf16 for r in which}
        else:
            ins |= first
            outs = {"out": shape((modes * rows, width), F32)}
        body = functools.partial(step, rows, which, moves, keys, halos, ends, second)
        env.update(call(body, ins, outs, flops=2 * modes * modes * width * len(keys)))

    env["inner"] = within_pair(env["q0"])
    env |= call(
        functools.partial(begin, rows),
        {"octant": octant.reshape(1, modes), "courant": courant, "collision": collision}
        | {f"p{r}": env[f"p{r}"] for r in range(rows)},
        {"c": shape(collision.shape, BF16), "coef": shape((modes, 8), F32)} | {f"sum{r}": row_f32 for r in range(rows)},
        hbm=("octant", "courant", "collision"),
        scratch=[pltpu.VMEM((1, modes), jnp.int32), pltpu.VMEM(courant.shape, F32), pltpu.SemaphoreType.DMA((3,))],
    )
    blocks = [exchange(env[f"q{r}"], orders[r][::-1], count, env["c"] if r == 0 else None) for r in range(rows)]
    env["outer"] = between_pairs(held(env[f"q{last}"], env["inner"]))
    run(blocks, range(rows), False, near, ["inner"], False, False)
    if last:
        run(blocks, range(last), False, [k for k in far if k[1] < last], [], True, False)
    run(blocks, range(last, rows), False, [k for k in far if k[1] == last], ["outer"], True, False)

    env["inner"] = within_pair(env["q0"])
    blocks = [exchange(env[f"q{r}"], orders[r], count) for r in range(rows)]
    env["outer"] = between_pairs(held(env[f"q{last}"], env["inner"]))
    run(blocks, range(rows), True, near, ["inner"], False, True)
    run(blocks, range(rows), False, far, ["outer"], True, True)
    return env["out"].reshape(populations.shape)


def solution(mesh):
    placed = (
        P("mode", None, "cell", None),
        P(None, "cell", None),
        P("mode"),
        P(None, "mode"),
        P("mode", None),
    )
    return jax.shard_map(
        on_device,
        mesh=mesh,
        in_specs=placed,
        out_specs=P("mode", None, "cell", None),
        check_vma=False,
    )
```

```python
import functools

import jax
import jax.numpy as jnp
from jax import lax
from jax.experimental import pallas as pl
from jax.experimental.pallas import tpu as pltpu
from jax.sharding import PartitionSpec as P

F32 = jnp.float32
BF16 = jnp.bfloat16
ANY = pl.BlockSpec(memory_space=pl.ANY)
HBM = pl.BlockSpec(memory_space=pltpu.HBM)
VMEM = pl.BlockSpec(memory_space=pltpu.VMEM)


def shape(dims, dtype):
    return jax.ShapeDtypeStruct(dims, dtype)


def call(body, ins, outs, hbm=(), after=(), scratch=(), flops=0):
    names, out_names = list(ins), list(outs)
    args = [pltpu.with_memory_space_constraint(ins[n], pltpu.HBM) if n in hbm else ins[n] for n in names]
    args += list(after)
    total = sum(a.size * a.dtype.itemsize for a in (*outs.values(), *args))

    def kernel(*refs):
        a, b = len(args), len(args) + len(outs)
        body(dict(zip(names, refs)), dict(zip(out_names, refs[a:b])), *refs[b:])

    results = pl.pallas_call(
        kernel,
        out_shape=list(outs.values()),
        in_specs=[HBM if n in hbm else VMEM for n in names] + [ANY] * len(after),
        out_specs=[VMEM] * len(outs),
        scratch_shapes=list(scratch),
        compiler_params=pltpu.CompilerParams(vmem_limit_bytes=24 * 2**20),
        cost_estimate=pl.CostEstimate(flops=flops, bytes_accessed=total, transcendentals=0),
    )(*args)
    return dict(zip(out_names, results))


def is_first():
    return 1 - lax.axis_index("cell") % 2


def turned(values):
    first = is_first() == 1
    return [jnp.where(first, other, value) for value, other in zip(values, values[::-1])]


def prepare(rows, ins, outs, pop, mask, sems):
    copies = [
        pltpu.make_async_copy(ins["mask"], mask, sems.at[0]),
        pltpu.make_async_copy(ins["pop"], pop, sems.at[1]),
    ]
    for copy in copies:
        copy.start()
    for copy in copies:
        copy.wait()
    modes = outs["p0"].shape[0]
    keeps = turned([(1 - mask[r : r + 1, :]).astype(F32) for r in range(rows)])
    fields = turned([pop[pl.ds(r, modes, stride=rows), :] for r in range(rows)])
    for r, (keep, field) in enumerate(zip(keeps, fields)):
        row = keep * field
        outs["keep"][r : r + 1, :] = keep
        outs[f"p{r}"][...] = row
        outs[f"q{r}"][...] = row.astype(BF16)


def coefficients(octant, courant):
    speeds = [(1.0 - 2.0 * ((octant >> d) & 1).astype(F32)) * courant[d : d + 1] for d in range(3)]
    flags = [(v < 0).astype(F32) for v in speeds]
    return jnp.concatenate([jnp.abs(v) for v in speeds] + flags + flags[:2], axis=0).T


def backward_y(coef):
    return (coef[:, 4:5] > 0) == (is_first() == 0)


def drift(fields, r, coef):
    p = fields[r]
    width = p.shape[1]
    ax, ay, az = (coef[:, d : d + 1] for d in range(3))
    beside = jnp.where(coef[:, 3:4] > 0, pltpu.roll(p, width - 1, 1), pltpu.roll(p, 1, 1))
    prior = fields[r - 1] if r > 0 else jnp.zeros_like(p)
    later = fields[r + 1] if r < len(fields) - 1 else jnp.zeros_like(p)
    return (1.0 - (ax + ay + az)) * p + ax * beside + ay * jnp.where(backward_y(coef), later, prior)


def mirrored(offset, count):
    bits = count.bit_length() - 1
    return sum((offset >> b & 1) << (bits - 1 - b) for b in range(bits))


def product(c, offset, blocks):
    modes = blocks[0].shape[0]
    other = mirrored(offset, c.shape[1] // modes)
    position = lax.axis_index("mode") ^ (is_first() * offset + (1 - is_first()) * other)
    cols = pl.ds(pl.multiple_of(position * modes, modes), modes)
    return jnp.dot(c[:, cols], jnp.concatenate(blocks, axis=1), preferred_element_type=F32)


def begin(rows, ins, outs, octant, courant, sems):
    copies = [
        pltpu.make_async_copy(ins["octant"], octant, sems.at[0]),
        pltpu.make_async_copy(ins["courant"], courant, sems.at[1]),
        pltpu.make_async_copy(ins["collision"], outs["c"], sems.at[2]),
    ]
    for copy in copies:
        copy.start()
    copies[0].wait()
    copies[1].wait()
    coef = coefficients(octant[...], courant[...])
    outs["coef"][...] = coef
    fields = [ins[f"p{r}"][...] for r in range(rows)]
    moved = [drift(fields, r, coef) for r in range(rows)]
    copies[2].wait()
    own = product(outs["c"], 0, [ins[f"q{r}"][...] for r in range(rows)])
    width = own.shape[1] // rows
    for r in range(rows):
        outs[f"sum{r}"][...] = moved[r] - own[:, r * width : (r + 1) * width]


def step(rows, which, moves, keys, halos, ends, second, ins, outs):
    values = {r: 0.0 if moves else ins[f"sum{r}"][...] for r in which}
    if moves:
        fields = [ins[f"p{r}"][...] for r in range(rows)]
        values = {r: drift(fields, r, ins["coef"]) for r in which}
    if "inner" in halos:
        values[0] += jnp.where(backward_y(ins["coef"]), 0.0, ins["coef"][:, 1:2] * ins["inner"][...].astype(F32))
    if "outer" in halos:
        values[rows - 1] += jnp.where(backward_y(ins["coef"]), ins["coef"][:, 1:2] * ins["outer"][...].astype(F32), 0.0)
    for offset in sorted({o for o, _ in keys}):
        having = [r for r in which if (offset, r) in keys]
        result = product(ins["c"], offset, [ins[f"b{offset}_{r}"][...] for r in having])
        width = result.shape[1] // len(having)
        for i, r in enumerate(having):
            values[r] = values[r] - result[:, i * width : (i + 1) * width]
    if ends and second:
        modes = outs["out"].shape[0] // rows
        last = [ins["keep"][r : r + 1] * (0.5 * ins[f"first{r}"][...] + 0.5 * values[r]) for r in range(rows)]
        for r, value in enumerate(turned(last)):
            outs["out"][pl.ds(r, modes, stride=rows), :] = value
        return
    for r, value in values.items():
        if ends:
            value = ins["keep"][r : r + 1] * value
            outs[f"p{r}"][...] = value
            outs[f"q{r}"][...] = value.astype(BF16)
        else:
            outs[f"sum{r}"][...] = value


def held(row, other):
    def body(ins, outs):
        outs["row"][...] = ins["row"][...]

    return call(body, {"row": row}, {"row": shape(row.shape, row.dtype)}, after=[other])["row"]


def exchange(row, bits, count, other=None):
    cells = lax.axis_size("cell")
    blocks = {0: row}
    for i, bit in enumerate(bits):
        both = bit, mirrored(bit, count)
        pairs = [(m * cells + c, (m ^ both[c % 2]) * cells + c) for m in range(count) for c in range(cells)]
        for offset, block in list(blocks.items()):
            if i and offset and other is not None:
                block = held(block, other)
            blocks[offset ^ bit] = lax.ppermute(block, ("mode", "cell"), pairs)
    return blocks


def within_pair(row):
    return lax.ppermute(row, "cell", [(i, i ^ 1) for i in range(lax.axis_size("cell"))])


def between_pairs(row):
    steps = [(i, i + 1) for i in range(1, lax.axis_size("cell") - 1, 2)]
    return lax.ppermute(row, "cell", steps + [(target, source) for source, target in steps])


def on_device(populations, contact_mask, octant, courant, collision):
    modes, planes, rows, width = populations.shape
    count = lax.axis_size("mode")
    assert planes == 1 and lax.axis_size("cell") % 2 == 0 and count & (count - 1) == 0
    last = rows - 1
    bits = [1 << b for b in range(count.bit_length() - 1)]
    orders = [bits if r % 2 == 0 else bits[::-1] for r in range(rows)]
    row_f32, row_bf16 = shape((modes, width), F32), shape((modes, width), BF16)
    keys = [(o, r) for r in range(rows) for o in range(count)]
    near = [(o, r) for o, r in keys if o == 0 or o in bits]
    far = [key for key in keys if key not in near]

    pop, mask = populations.reshape(modes * rows, width), contact_mask.reshape(rows, width)
    outs = {"keep": shape((rows, width), F32)}
    for r in range(rows):
        outs |= {f"p{r}": row_f32, f"q{r}": row_bf16}
    env = call(
        functools.partial(prepare, rows),
        {"pop": pop, "mask": mask},
        outs,
        hbm=("pop", "mask"),
        scratch=[pltpu.VMEM(pop.shape, F32), pltpu.VMEM(mask.shape, jnp.int32), pltpu.SemaphoreType.DMA((2,))],
    )
    first = {f"first{r}": env[f"p{r}"] for r in range(rows)}

    def run(blocks, which, moves, keys, halos, ends, second):
        names = [f"p{r}" for r in range(rows)] if moves else [f"sum{r}" for r in which]
        names += [*halos] + ["coef"] * (moves or len(halos) > 0) + ["c"] * (len(keys) > 0) + ["keep"] * ends
        ins = {n: env[n] for n in names} | {f"b{o}_{r}": blocks[r][o] for o, r in keys}
        if not ends:
            outs = {f"sum{r}": row_f32 for r in which}
        elif not second:
            outs = {f"p{r}": row_f32 for r in which} | {f"q{r}": row_bf16 for r in which}
        else:
            ins |= first
            outs = {"out": shape((modes * rows, width), F32)}
        body = functools.partial(step, rows, which, moves, keys, halos, ends, second)
        env.update(call(body, ins, outs, flops=2 * modes * modes * width * len(keys)))

    env["inner"] = within_pair(env["q0"])
    env |= call(
        functools.partial(begin, rows),
        {"octant": octant.reshape(1, modes), "courant": courant, "collision": collision}
        | {f"{n}{r}": env[f"{n}{r}"] for n in "pq" for r in range(rows)},
        {"c": shape(collision.shape, BF16), "coef": shape((modes, 8), F32)} | {f"sum{r}": row_f32 for r in range(rows)},
        hbm=("octant", "courant", "collision"),
        scratch=[pltpu.VMEM((1, modes), jnp.int32), pltpu.VMEM(courant.shape, F32), pltpu.SemaphoreType.DMA((3,))],
    )
    blocks = [exchange(env[f"q{r}"], orders[r][::-1], count, env["c"] if r == 0 else None) for r in range(rows)]
    env["outer"] = between_pairs(held(env[f"q{last}"], env["inner"]))
    run(blocks, range(rows), False, [key for key in near if key[0]], ["inner"], False, False)
    if last:
        run(blocks, range(last), False, [k for k in far if k[1] < last], [], True, False)
    run(blocks, range(last, rows), False, [k for k in far if k[1] == last], ["outer"], True, False)

    env["inner"] = within_pair(env["q0"])
    blocks = [exchange(env[f"q{r}"], orders[r], count) for r in range(rows)]
    env["outer"] = between_pairs(held(env[f"q{last}"], env["inner"]))
    run(blocks, range(rows), True, near, ["inner"], False, True)
    run(blocks, range(rows), False, far, ["outer"], True, True)
    return env["out"].reshape(populations.shape)


def solution(mesh):
    placed = (
        P("mode", None, "cell", None),
        P(None, "cell", None),
        P("mode"),
        P(None, "mode"),
        P("mode", None),
    )
    return jax.shard_map(
        on_device,
        mesh=mesh,
        in_specs=placed,
        out_specs=P("mode", None, "cell", None),
        check_vma=False,
    )
```

```python
import functools

import jax
import jax.numpy as jnp
from jax import lax
from jax.experimental import pallas as pl
from jax.experimental.pallas import tpu as pltpu
from jax.sharding import PartitionSpec as P

F32 = jnp.float32
BF16 = jnp.bfloat16
ANY = pl.BlockSpec(memory_space=pl.ANY)
HBM = pl.BlockSpec(memory_space=pltpu.HBM)
VMEM = pl.BlockSpec(memory_space=pltpu.VMEM)


def shape(dims, dtype):
    return jax.ShapeDtypeStruct(dims, dtype)


def call(body, ins, outs, hbm=(), after=(), scratch=(), flops=0):
    names, out_names = list(ins), list(outs)
    args = [pltpu.with_memory_space_constraint(ins[n], pltpu.HBM) if n in hbm else ins[n] for n in names]
    args += list(after)
    total = sum(a.size * a.dtype.itemsize for a in (*outs.values(), *args))

    def kernel(*refs):
        a, b = len(args), len(args) + len(outs)
        body(dict(zip(names, refs)), dict(zip(out_names, refs[a:b])), *refs[b:])

    results = pl.pallas_call(
        kernel,
        out_shape=list(outs.values()),
        in_specs=[HBM if n in hbm else VMEM for n in names] + [ANY] * len(after),
        out_specs=[VMEM] * len(outs),
        scratch_shapes=list(scratch),
        compiler_params=pltpu.CompilerParams(vmem_limit_bytes=24 * 2**20),
        cost_estimate=pl.CostEstimate(flops=flops, bytes_accessed=total, transcendentals=0),
    )(*args)
    return dict(zip(out_names, results))


def is_first():
    return 1 - lax.axis_index("cell") % 2


def turned(values):
    first = is_first() == 1
    return [jnp.where(first, other, value) for value, other in zip(values, values[::-1])]


def prepare(rows, ins, outs, pop, mask, sems):
    copies = [
        pltpu.make_async_copy(ins["mask"], mask, sems.at[0]),
        pltpu.make_async_copy(ins["pop"], pop, sems.at[1]),
    ]
    for copy in copies:
        copy.start()
    for copy in copies:
        copy.wait()
    modes = outs["p0"].shape[0]
    keeps = turned([(1 - mask[r : r + 1, :]).astype(F32) for r in range(rows)])
    fields = turned([pop[pl.ds(r, modes, stride=rows), :] for r in range(rows)])
    for r, (keep, field) in enumerate(zip(keeps, fields)):
        row = keep * field
        outs["keep"][r : r + 1, :] = keep
        outs[f"p{r}"][...] = row
        outs[f"q{r}"][...] = row.astype(BF16)


def coefficients(octant, courant):
    speeds = [(1.0 - 2.0 * ((octant >> d) & 1).astype(F32)) * courant[d : d + 1] for d in range(3)]
    flags = [(v < 0).astype(F32) for v in speeds]
    return jnp.concatenate([jnp.abs(v) for v in speeds] + flags + flags[:2], axis=0).T


def backward_y(coef):
    return (coef[:, 4:5] > 0) == (is_first() == 0)


def drift(fields, r, coef):
    p = fields[r]
    width = p.shape[1]
    ax, ay, az = (coef[:, d : d + 1] for d in range(3))
    beside = jnp.where(coef[:, 3:4] > 0, pltpu.roll(p, width - 1, 1), pltpu.roll(p, 1, 1))
    prior = fields[r - 1] if r > 0 else jnp.zeros_like(p)
    later = fields[r + 1] if r < len(fields) - 1 else jnp.zeros_like(p)
    return (1.0 - (ax + ay + az)) * p + ax * beside + ay * jnp.where(backward_y(coef), later, prior)


def mirrored(offset, count):
    bits = count.bit_length() - 1
    return sum((offset >> b & 1) << (bits - 1 - b) for b in range(bits))


def product(c, offset, blocks):
    modes = blocks[0].shape[0]
    other = mirrored(offset, c.shape[1] // modes)
    position = lax.axis_index("mode") ^ (is_first() * offset + (1 - is_first()) * other)
    cols = pl.ds(pl.multiple_of(position * modes, modes), modes)
    return jnp.dot(c[:, cols], jnp.concatenate(blocks, axis=1), preferred_element_type=F32)


def begin(rows, ins, outs, octant, courant, sems):
    copies = [
        pltpu.make_async_copy(ins["octant"], octant, sems.at[0]),
        pltpu.make_async_copy(ins["courant"], courant, sems.at[1]),
        pltpu.make_async_copy(ins["collision"], outs["c"], sems.at[2]),
    ]
    for copy in copies:
        copy.start()
    copies[0].wait()
    copies[1].wait()
    coef = coefficients(octant[...], courant[...])
    outs["coef"][...] = coef
    fields = [ins[f"p{r}"][...] for r in range(rows)]
    for r in range(rows):
        outs[f"sum{r}"][...] = drift(fields, r, coef)
    copies[2].wait()


def step(rows, which, moves, keys, halos, ends, second, ins, outs):
    values = {r: 0.0 if moves else ins[f"sum{r}"][...] for r in which}
    if moves:
        fields = [ins[f"p{r}"][...] for r in range(rows)]
        values = {r: drift(fields, r, ins["coef"]) for r in which}
    if "inner" in halos:
        values[0] += jnp.where(backward_y(ins["coef"]), 0.0, ins["coef"][:, 1:2] * ins["inner"][...].astype(F32))
    if "outer" in halos:
        values[rows - 1] += jnp.where(backward_y(ins["coef"]), ins["coef"][:, 1:2] * ins["outer"][...].astype(F32), 0.0)
    for offset in sorted({o for o, _ in keys}):
        having = [r for r in which if (offset, r) in keys]
        result = product(ins["c"], offset, [ins[f"b{offset}_{r}"][...] for r in having])
        width = result.shape[1] // len(having)
        for i, r in enumerate(having):
            values[r] = values[r] - result[:, i * width : (i + 1) * width]
    if ends and second:
        modes = outs["out"].shape[0] // rows
        last = [ins["keep"][r : r + 1] * (0.5 * ins[f"first{r}"][...] + 0.5 * values[r]) for r in range(rows)]
        for r, value in enumerate(turned(last)):
            outs["out"][pl.ds(r, modes, stride=rows), :] = value
        return
    for r, value in values.items():
        if ends:
            value = ins["keep"][r : r + 1] * value
            outs[f"p{r}"][...] = value
            outs[f"q{r}"][...] = value.astype(BF16)
        else:
            outs[f"sum{r}"][...] = value


def held(row, other):
    def body(ins, outs):
        outs["row"][...] = ins["row"][...]

    return call(body, {"row": row}, {"row": shape(row.shape, row.dtype)}, after=[other])["row"]


def exchange(row, bits, count, other=None):
    cells = lax.axis_size("cell")
    blocks = {0: row}
    for i, bit in enumerate(bits):
        both = bit, mirrored(bit, count)
        pairs = [(m * cells + c, (m ^ both[c % 2]) * cells + c) for m in range(count) for c in range(cells)]
        for offset, block in list(blocks.items()):
            if i and offset and other is not None:
                block = held(block, other)
            blocks[offset ^ bit] = lax.ppermute(block, ("mode", "cell"), pairs)
    return blocks


def within_pair(row):
    return lax.ppermute(row, "cell", [(i, i ^ 1) for i in range(lax.axis_size("cell"))])


def between_pairs(row):
    steps = [(i, i + 1) for i in range(1, lax.axis_size("cell") - 1, 2)]
    return lax.ppermute(row, "cell", steps + [(target, source) for source, target in steps])


def on_device(populations, contact_mask, octant, courant, collision):
    modes, planes, rows, width = populations.shape
    count = lax.axis_size("mode")
    assert planes == 1 and lax.axis_size("cell") % 2 == 0 and count & (count - 1) == 0
    last = rows - 1
    bits = [1 << b for b in range(count.bit_length() - 1)]
    orders = [bits if r % 2 == 0 else bits[::-1] for r in range(rows)]
    row_f32, row_bf16 = shape((modes, width), F32), shape((modes, width), BF16)
    keys = [(o, r) for r in range(rows) for o in range(count)]
    near = [(o, r) for o, r in keys if o == 0 or o in bits]
    far = [key for key in keys if key not in near]

    pop, mask = populations.reshape(modes * rows, width), contact_mask.reshape(rows, width)
    outs = {"keep": shape((rows, width), F32)}
    for r in range(rows):
        outs |= {f"p{r}": row_f32, f"q{r}": row_bf16}
    env = call(
        functools.partial(prepare, rows),
        {"pop": pop, "mask": mask},
        outs,
        hbm=("pop", "mask"),
        scratch=[pltpu.VMEM(pop.shape, F32), pltpu.VMEM(mask.shape, jnp.int32), pltpu.SemaphoreType.DMA((2,))],
    )
    first = {f"first{r}": env[f"p{r}"] for r in range(rows)}

    def run(blocks, which, moves, keys, halos, ends, second):
        names = [f"p{r}" for r in range(rows)] if moves else [f"sum{r}" for r in which]
        names += [*halos] + ["coef"] * (moves or len(halos) > 0) + ["c"] * (len(keys) > 0) + ["keep"] * ends
        ins = {n: env[n] for n in names} | {f"b{o}_{r}": blocks[r][o] for o, r in keys}
        if not ends:
            outs = {f"sum{r}": row_f32 for r in which}
        elif not second:
            outs = {f"p{r}": row_f32 for r in which} | {f"q{r}": row_bf16 for r in which}
        else:
            ins |= first
            outs = {"out": shape((modes * rows, width), F32)}
        body = functools.partial(step, rows, which, moves, keys, halos, ends, second)
        env.update(call(body, ins, outs, flops=2 * modes * modes * width * len(keys)))

    env["inner"] = within_pair(env["q0"])
    env |= call(
        functools.partial(begin, rows),
        {"octant": octant.reshape(1, modes), "courant": courant, "collision": collision}
        | {f"p{r}": env[f"p{r}"] for r in range(rows)},
        {"c": shape(collision.shape, BF16), "coef": shape((modes, 8), F32)} | {f"sum{r}": row_f32 for r in range(rows)},
        hbm=("octant", "courant", "collision"),
        scratch=[pltpu.VMEM((1, modes), jnp.int32), pltpu.VMEM(courant.shape, F32), pltpu.SemaphoreType.DMA((3,))],
    )
    blocks = [exchange(env[f"q{r}"], orders[r][::-1], count, env["c"] if r == 0 else None) for r in range(rows)]
    env["outer"] = between_pairs(held(env[f"q{last}"], env["inner"]))
    run(blocks, range(rows), False, near, ["inner"], False, False)
    if last:
        run(blocks, range(last), False, [k for k in far if k[1] < last], [], True, False)
    run(blocks, range(last, rows), False, [k for k in far if k[1] == last], ["outer"], True, False)

    env["inner"] = within_pair(env["q0"])
    blocks = [exchange(env[f"q{r}"], orders[r], count, env["inner"] if r == last else None) for r in range(rows)]
    env["outer"] = between_pairs(held(env[f"q{last}"], env["inner"]))
    run(blocks, range(rows), True, near, ["inner"], False, True)
    run(blocks, range(rows), False, far, ["outer"], True, True)
    return env["out"].reshape(populations.shape)


def solution(mesh):
    placed = (
        P("mode", None, "cell", None),
        P(None, "cell", None),
        P("mode"),
        P(None, "mode"),
        P("mode", None),
    )
    return jax.shard_map(
        on_device,
        mesh=mesh,
        in_specs=placed,
        out_specs=P("mode", None, "cell", None),
        check_vma=False,
    )
```
